32 devices in a mesh: grid: 16 (over z, x, core), col: 2 (over y).
Axes of the slice: x: 2, y: 2, z: 4, core: 2. Of those that a mesh axis runs over, the one named last changes fastest.
Arguments:
- density: bfloat16 [16384, 16384], P('grid', 'col'), may hold values from -0.5 to 0.5
- centres: float32 [3, 16384], replicated, may hold values from -0.4 to 0.4
- exponents: float32 [16384], replicated, may hold values from 2 to 16
- coords: float32 [64, 3, 256], P('grid'), may hold values from -0.4 to 0.4
- weights: float32 [64, 256], P('grid'), may hold values from 0.078125 to 0.78125
- core_density: float32 [64, 256], P('grid'), may hold values from 0.3 to 3
- counts: int32 [64], P('grid'), may hold values from 1 to 256, 4096 in all
- blocks: int32 [64, 2], replicated, may hold values from 0 to 127, as said below
Outputs:
- potential_matrix_xc: float32 [16384, 16384], P('grid', 'col')
- orbital_charge_samples: float32 [64, 256], P('grid')
- xc_batch_amounts: float32 [64], P('grid')
The draws below stay inside these ranges and needn't reach their ends.
Inputs may be any that keep to these rules, and one draw needn't show every extreme that they name: Entry c of a batch's row names a block in the c-th of 2 equal runs of 64 blocks; for one grid index's 4 batches the values // 8 in one column c are distinct. The points in use are the first counts[b] slots.
All inputs are finite; a program needn't handle non-finite values. No bound on the sum of `counts` on one device may be relied on, other than what follows from the above.
Results may differ from the reference program's by a relative error of at most 0.0028.
Values may be sent and summed in bfloat16 or wider, within the bound.
A program may use at most 128 MiB of HBM per device.

```python
import math
import jax
import jax.numpy as jnp
import numpy as np
from jax import lax

NBF = 16384
BLK = 128
NB = 4
PTS = 256
RB = 8
BATCHES = 64
N_GRID = 16
N_COL = 2


def draw_blocks(key, part):
    groups_per = N_GRID // N_COL
    scores = jax.random.randint(key, (N_GRID, N_COL, groups_per), 0, 1 << 20)
    scores = scores * groups_per + jnp.arange(groups_per, dtype=jnp.int32)[None, None, :]
    ranking = jnp.argsort(scores, axis=2)[:, :, :NB].astype(jnp.int32)
    inner_rows = jax.random.randint(jax.random.fold_in(key, 7), (N_GRID, N_COL, NB), 0, RB)
    owner_grid = jnp.arange(N_COL, dtype=jnp.int32)[None, :, None] * groups_per + ranking
    chosen = owner_grid * RB + inner_rows
    return jnp.transpose(chosen, (0, 2, 1)).reshape(N_GRID * NB, N_COL).astype(jnp.int32)


def block_scale(key, dims, shards, low, high):
    level = 1.0
    for dim, shards_of in shards:
        steps = jax.random.uniform(jax.random.fold_in(jax.random.fold_in(key, 6), dim), (shards_of,), jnp.float32, low / len(shards), high / len(shards))
        level = level * jnp.repeat(jnp.exp(steps), dims[dim] // shards_of).reshape((-1,) + (1,) * (len(dims) - 1 - dim))
    return level


def profile(count, total, most, lean):
    weights = [(1 << 20) // math.isqrt(standing ** lean) + 1 for standing in range(2, count + 1)]
    spare, holding = total - most - (count - 1), [1] * (count - 1)
    while spare > 0:
        free = [i for i in range(count - 1) if holding[i] < most]
        mass, left = sum([weights[i] for i in free]), spare
        for i in free:
            extra = min(most - holding[i], max(1, left * weights[i] // mass), spare)
            holding[i] = holding[i] + extra
            spare = spare - extra
    return np.array([most] + holding)


def ragged_sizes(rng, number_of, total, limit, slope):
    if number_of == 2:
        one = jax.random.randint(rng, (), max(1, total - limit), min(limit, total - 1) + 1)
        return jnp.stack([one, total - one])
    sizes = jnp.asarray(profile(number_of, total, limit, slope), jnp.int32)
    couples = (number_of - 1) // 2
    donor, taker = sizes[1:1 + 2 * couples:2], sizes[2:2 + 2 * couples:2]
    room = jnp.minimum(donor - 1, limit - taker)
    moved = jax.random.randint(jax.random.fold_in(rng, 1), (couples,), 0, 1 << 20) % (room + 1)
    sizes = sizes.at[1:1 + 2 * couples:2].set(donor - moved).at[2:2 + 2 * couples:2].set(taker + moved)
    return sizes[jax.random.permutation(jax.random.fold_in(rng, 2), number_of)]


def noise(own_key, extent, width, most, pieces=(), held_as=jnp.bfloat16):
    drawn = width * jax.random.normal(own_key, extent, jnp.float32)
    if pieces:
        drawn = drawn * block_scale(own_key, extent, pieces, -0.22, 0.18)
    return jnp.clip(drawn, -most, most).astype(held_as)


def setup_inputs(seed: int = 0) -> dict:
    key_list = jax.random.split(jax.random.key(seed), 9)
    density = noise(key_list[0], (NBF, NBF), (20.0 / (N_COL * BLK)), 0.5, ((0, 16), (1, 2)))
    centres = jnp.clip(jax.random.uniform(key_list[1], (3, NBF), jnp.float32, -0.4, 0.4), -0.4, 0.4)
    exponents = jnp.clip(jnp.exp(jax.random.uniform(key_list[2], (NBF,), jnp.float32, math.log(2.0), math.log(16.0))), 2.0, 16.0)
    coords = jnp.clip(jax.random.uniform(key_list[3], (BATCHES, 3, PTS), jnp.float32, -0.4, 0.4) * block_scale(key_list[3], (BATCHES, 3, PTS), ((0, 16),), -0.4, 0.0), -0.4, 0.4)
    weights = jnp.clip(jnp.exp(math.log(0.78125) - 2.3025851 * jax.random.uniform(key_list[4], (BATCHES, PTS), jnp.float32) ** block_scale(key_list[4], (BATCHES, PTS), ((0, 16),), -0.2, 0.2)), 0.078125, 0.78125)
    core_density = jnp.clip(jnp.exp(math.log(3.0) - 2.3025851 * jax.random.uniform(key_list[5], (BATCHES, PTS), jnp.float32) ** block_scale(key_list[5], (BATCHES, PTS), ((0, 16),), -0.2, 0.2)), 0.3, 3.0)
    counts = ragged_sizes(key_list[6], BATCHES, BATCHES * PTS // 4, PTS, 2).astype(jnp.int32)
    blocks = draw_blocks(jax.random.fold_in(key_list[8], 71), 0)
    return dict(density=density, centres=centres, exponents=exponents, coords=coords, weights=weights, core_density=core_density, counts=counts, blocks=blocks)


kappa_pbe = 0.804
mu_coef = 0.2195
slater = -0.7385587663820224
grad_scale = 4.0 * (3.0 * math.pi ** 2) ** (2.0 / 3.0)
soft_square = 0.25

def pbe_energy(total, grad_square):
    regular = 0.5 * (total + jnp.sqrt(total * total + soft_square))
    scaled = grad_scale * jnp.power(regular, 8.0 / 3.0)
    enhance = 1.0 + kappa_pbe - kappa_pbe * kappa_pbe * scaled / (kappa_pbe * scaled + mu_coef * grad_square)
    return slater * jnp.power(regular, 4.0 / 3.0) * enhance

def xc_kernel(total, grad_square):
    total_functional_sum, pullback = jax.vjp(pbe_energy, total, grad_square)
    charge_derivative, deriv_sigma = pullback(jnp.ones_like(total_functional_sum))
    return (total_functional_sum, charge_derivative, deriv_sigma)

def basis(points, centre_rows, rate_rows):
    offset = points[:, :, None] - centre_rows[:, None, :]
    distance = lax.optimization_barrier(jnp.sum(offset * offset, axis=0))
    value_entries = jnp.exp(-rate_rows[None, :] * distance)
    slopes = -2.0 * rate_rows[None, None, :] * offset * value_entries[None]
    return (value_entries, slopes)

def reference(density, centres, exponents, coords, weights, core_density, counts, blocks):
    offsets = jnp.arange(BLK, dtype=jnp.int32)
    point_ids = jnp.arange(PTS, dtype=jnp.int32)

    def one_batch(matrix, inputs):
        points, point_weights, core, count, block_row = inputs
        func_index = (block_row[:, None] * BLK + offsets[None, :]).reshape(-1).astype(jnp.int32)
        value_entries, slopes = basis(points, jnp.take(centres, func_index, axis=1), jnp.take(exponents, func_index))
        sub_matrix = jnp.take(jnp.take(density, func_index, axis=0), func_index, axis=1)
        phi_low = value_entries.astype(jnp.bfloat16)
        right_sum = jnp.dot(phi_low, sub_matrix, preferred_element_type=jnp.float32)
        left_sum = lax.dot_general(phi_low, sub_matrix, (((1,), (1,)), ((), ())), preferred_element_type=jnp.float32)
        live_mask = (point_ids < count).astype(jnp.float32)
        valence = live_mask * lax.optimization_barrier(jnp.sum(value_entries * right_sum, axis=1))
        gradient = live_mask[None, :] * (lax.optimization_barrier(jnp.sum(slopes * left_sum[None], axis=2)) + lax.optimization_barrier(jnp.sum(slopes * right_sum[None], axis=2)))
        grad_square = lax.optimization_barrier(jnp.sum(gradient * gradient, axis=0))
        total_functional_sum, charge_derivative, deriv_sigma = xc_kernel(valence + core, grad_square)
        point_scale = point_weights * live_mask
        fweight = point_scale * charge_derivative
        hweight = (2.0 * point_scale * deriv_sigma)[None, :] * gradient
        batch_energy = jnp.sum(point_scale * total_functional_sum)
        across = lax.optimization_barrier(jnp.sum(hweight[:, :, None] * slopes, axis=0))
        along = fweight[:, None] * value_entries + across
        left_side = jnp.concatenate([phi_low, across.astype(jnp.bfloat16)], axis=0)
        right_side = jnp.concatenate([along.astype(jnp.bfloat16), phi_low], axis=0)
        block_result_value = lax.dot_general(left_side, right_side, (((0,), (0,)), ((), ())), preferred_element_type=jnp.float32)
        matrix = matrix.at[func_index[:, None], func_index[None, :]].add(block_result_value)
        return (matrix, (valence, batch_energy))
    start = jnp.zeros((NBF, NBF), jnp.float32)
    matrix, (valence_all, energy_all) = lax.scan(one_batch, start, (coords, weights, core_density, counts, blocks))
    return (matrix, valence_all, energy_all)
```

```python
import math

import jax
import jax.numpy as jnp
from jax import lax
from jax.experimental import pallas as pl
from jax.experimental.pallas import tpu as pltpu
from jax.sharding import PartitionSpec as P

BLK = 128
FILL_ROWS = 32
FIRST_FILL = 0.5
VMEM_LIMIT = 48 * 1024 * 1024
MESH = pl.DeviceIdType.MESH
F32 = jnp.float32
BF16 = jnp.bfloat16

kappa_pbe = 0.804
mu_coef = 0.2195
slater = -0.7385587663820224
grad_scale = 4.0 * (3.0 * math.pi**2) ** (2.0 / 3.0)
soft_square = 0.25


def xc_kernel(total, grad_square):
    root = jnp.sqrt(total * total + soft_square)
    regular = 0.5 * (total + root)
    log_regular = jnp.log(regular)
    third = jnp.exp(log_regular * (1.0 / 3.0))
    four_thirds = jnp.exp(log_regular * (4.0 / 3.0))
    scaled = grad_scale * four_thirds * four_thirds
    inverse = 1.0 / (kappa_pbe * scaled + mu_coef * grad_square)
    ratio = scaled * inverse
    enhance = 1.0 + kappa_pbe - kappa_pbe * kappa_pbe * ratio
    energy = slater * four_thirds * enhance
    inner = (4.0 / 3.0) * enhance - (8.0 / 3.0) * kappa_pbe * kappa_pbe * ratio * (
        mu_coef * grad_square * inverse
    )
    deriv_density = slater * third * inner * (0.5 * (1.0 + total / root))
    deriv_sigma = slater * four_thirds * (kappa_pbe * kappa_pbe * mu_coef) * ratio * inverse
    return energy, deriv_density, deriv_sigma


def parts_of(value):
    first = value.astype(BF16).astype(F32)
    rest = value - first
    second = rest.astype(BF16).astype(F32)
    return first, second, rest - second


def outer_sum(left, right):
    l1, l2, l3 = parts_of(left)
    r1, r2, r3 = parts_of(right)
    lefts = jnp.concatenate([l1, l1, l1, l2, l2, l3], axis=0).astype(BF16)
    rights = jnp.concatenate([r1, r2, r3, r1, r2, r1], axis=0).astype(BF16)
    return lax.dot_general(
        lefts, rights, (((0,), (0,)), ((), ())), preferred_element_type=F32
    )


def batch_of(blocks_ref, requester, entry, owner, batches, row_blocks):
    found = jnp.int32(-1)
    for batch in range(batches):
        block = blocks_ref[requester * batches + batch, entry]
        found = jnp.where(lax.div(block, row_blocks) == owner, batch, found)
    return found


def exchange_points(sizes, blocks_ref, counts_ref, coords_ref, out_ref, staged, landed, send, recv):
    grid_size, col_size, batches, row_blocks, halves = sizes
    me, col = lax.axis_index("grid"), lax.axis_index("col")
    barrier = pltpu.get_barrier_semaphore()
    for step in range(1, grid_size):
        other = lax.rem(me + step, grid_size)
        pl.semaphore_signal(barrier, inc=1, device_id=(other, col), device_id_type=MESH)
    group = grid_size // col_size
    for owner in range(grid_size):
        batch = jnp.maximum(
            batch_of(blocks_ref, me, owner // group, owner, batches, row_blocks), 0
        )
        points = coords_ref[batch]
        count = jnp.full((1, BLK), counts_ref[batch].astype(F32), F32)
        pieces = []
        for half in range(halves):
            pieces += [points[:, half * BLK : (half + 1) * BLK], count]
        staged[owner] = jnp.concatenate(pieces, axis=0)
    pl.semaphore_wait(barrier, grid_size - 1)
    copies = []
    for step in range(1, grid_size):
        other = lax.rem(me + step, grid_size)
        copy = pltpu.make_async_remote_copy(
            src_ref=staged.at[other],
            dst_ref=landed.at[me],
            send_sem=send.at[step],
            recv_sem=recv.at[step],
            device_id=(other, col),
            device_id_type=MESH,
        )
        copy.start()
        copies.append(copy)
    landed[me] = staged[me]
    for copy in copies:
        copy.wait()
    out_ref[...] = landed[...]


def exchange_sums(
    sizes,
    blocks_ref,
    counts_ref,
    sums_ref,
    weights_ref,
    core_ref,
    out_ref,
    extra_ref,
    landed,
    col_sums,
    fields,
    staged,
    returned,
    send_a,
    recv_a,
    send_b,
    recv_b,
    send_c,
    recv_c,
):
    grid_size, col_size, batches, row_blocks, halves = sizes
    me, col = lax.axis_index("grid"), lax.axis_index("col")
    barrier = pltpu.get_barrier_semaphore()
    for step in range(1, grid_size):
        other = lax.rem(me + step, grid_size)
        pl.semaphore_signal(barrier, inc=1, device_id=(other, col), device_id_type=MESH)
    for step in range(1, col_size):
        other = lax.rem(col + step, col_size)
        pl.semaphore_signal(barrier, inc=1, device_id=(me, other), device_id_type=MESH)
    pl.semaphore_wait(barrier, grid_size + col_size - 2)

    copies = []
    for step in range(1, grid_size):
        other = lax.rem(me + step, grid_size)
        copy = pltpu.make_async_remote_copy(
            src_ref=sums_ref.at[other],
            dst_ref=landed.at[me],
            send_sem=send_a.at[step],
            recv_sem=recv_a.at[step],
            device_id=(other, col),
            device_id_type=MESH,
        )
        copy.start()
        copies.append(copy)
    landed[me] = sums_ref[me]
    for copy in copies:
        copy.wait()

    for batch in range(batches):
        total = None
        for entry in range(col_size):
            owner = lax.div(blocks_ref[me * batches + batch, entry], row_blocks)
            term = landed[owner]
            total = term if total is None else total + term
        col_sums[col, batch] = total
    copies = []
    for step in range(1, col_size):
        other = lax.rem(col + step, col_size)
        copy = pltpu.make_async_remote_copy(
            src_ref=col_sums.at[col],
            dst_ref=col_sums.at[col],
            send_sem=send_b.at[step],
            recv_sem=recv_b.at[step],
            device_id=(me, other),
            device_id_type=MESH,
        )
        copy.start()
        copies.append(copy)
    for copy in copies:
        copy.wait()
    summed = col_sums[0]
    for entry in range(1, col_size):
        summed = summed + col_sums[entry]

    places = [(batch, half) for batch in range(batches) for half in range(halves)]

    def rows_of(field):
        return jnp.concatenate(
            [summed[batch, 4 * half + field : 4 * half + field + 1] for batch, half in places],
            axis=0,
        )

    def rows_in(ref):
        value = ref[...]
        return jnp.concatenate(
            [value[batch : batch + 1, half * BLK : (half + 1) * BLK] for batch, half in places],
            axis=0,
        )

    lanes = lax.broadcasted_iota(jnp.int32, (1, BLK), 1)
    live = jnp.concatenate(
        [jnp.where(lanes + half * BLK < counts_ref[batch], 1.0, 0.0) for batch, half in places],
        axis=0,
    )
    valence = jnp.where(live > 0.0, rows_of(0), 0.0)
    gradient = [jnp.where(live > 0.0, rows_of(1 + d), 0.0) for d in range(3)]
    grad_square = (
        gradient[0] * gradient[0] + gradient[1] * gradient[1] + gradient[2] * gradient[2]
    )
    energy, deriv_density, deriv_sigma = xc_kernel(valence + rows_in(core_ref), grad_square)
    point_scale = rows_in(weights_ref) * live
    spread = 2.0 * point_scale * deriv_sigma
    table = [point_scale * deriv_density] + [spread * gradient[d] for d in range(3)]
    for batch in range(batches):
        fields[batch] = jnp.concatenate(
            [
                table[k][batch * halves + half : batch * halves + half + 1]
                for half in range(halves)
                for k in range(4)
            ],
            axis=0,
        )
    group = grid_size // col_size
    for owner in range(grid_size):
        batch = jnp.maximum(
            batch_of(blocks_ref, me, owner // group, owner, batches, row_blocks), 0
        )
        staged[owner] = fields[batch]
    copies = []
    for step in range(1, grid_size):
        other = lax.rem(me + step, grid_size)
        copy = pltpu.make_async_remote_copy(
            src_ref=staged.at[other],
            dst_ref=returned.at[me],
            send_sem=send_c.at[step],
            recv_sem=recv_c.at[step],
            device_id=(other, col),
            device_id_type=MESH,
        )
        copy.start()
        copies.append(copy)
    returned[me] = staged[me]
    extra_ref[0] = valence
    extra_ref[1] = point_scale * energy
    for copy in copies:
        copy.wait()
    out_ref[...] = returned[...]


def list_tiles(sizes, blocks_ref, points_ref, tile_slot, tile_row, tile_col, item_tile, item_half):
    grid_size, col_size, batches, row_blocks, halves = sizes
    me, col = lax.axis_index("grid"), lax.axis_index("col")
    entry = lax.div(me, grid_size // col_size)

    def step(slot, carry):
        tiles, items = carry
        found = batch_of(blocks_ref, slot, entry, me, batches, row_blocks)
        batch = jnp.maximum(found, 0)
        has = found >= 0
        tile_slot[tiles] = slot
        tile_row[tiles] = blocks_ref[slot * batches + batch, entry]
        tile_col[tiles] = blocks_ref[slot * batches + batch, col]
        count = points_ref[slot, 3, 0]
        for half in range(halves):
            item_tile[items] = tiles
            item_half[items] = half
            items = items + jnp.where(has & (count > half * BLK), 1, 0)
        return tiles + jnp.where(has, 1, 0), items

    return lax.fori_loop(0, grid_size, step, (jnp.int32(0), jnp.int32(0)))


def half_rows(value, half, halves):
    picked = value[0:4]
    for other in range(1, halves):
        picked = jnp.where(half == other, value[4 * other : 4 * other + 4], picked)
    return picked


def functions_of(centres_ref, exponents_ref, row, column):
    rate = jnp.concatenate(
        [exponents_ref[pl.ds(row, 1), :], exponents_ref[pl.ds(column, 1), :]], axis=1
    )
    centre = jnp.concatenate(
        [
            centres_ref[:, pl.ds(pl.multiple_of(row * BLK, BLK), BLK)],
            centres_ref[:, pl.ds(pl.multiple_of(column * BLK, BLK), BLK)],
        ],
        axis=1,
    )
    return rate, centre


def basis(points, rate, centre):
    square = jnp.sum(points * points, axis=0, keepdims=True)
    none = jnp.zeros((3, BLK), F32)
    right = jnp.concatenate([square, points, jnp.ones((1, BLK), F32), none], axis=0)
    left = jnp.concatenate(
        [
            -rate,
            2.0 * rate * centre,
            -rate * jnp.sum(centre * centre, axis=0, keepdims=True),
            jnp.zeros((3, 2 * BLK), F32),
        ],
        axis=0,
    )
    return jnp.exp(outer_sum(left, right))


def coefficients(rate, centre):
    lanes = lax.broadcasted_iota(jnp.int32, (1, 2 * BLK), 1)
    return jnp.concatenate(
        [
            rate,
            rate * centre,
            jnp.where(lanes >= BLK, 1.0, 0.0),
            jnp.zeros((3, 2 * BLK), F32),
        ],
        axis=0,
    )


def density_tiles(
    sizes,
    fills,
    blocks_ref,
    points_ref,
    density_ref,
    centres_ref,
    exponents_ref,
    sums_ref,
    matrix_ref,
    held,
    zeros,
    tile_slot,
    tile_row,
    tile_col,
    item_tile,
    item_half,
    tile_sem,
    fill_sem,
):
    grid_size, col_size, batches, row_blocks, halves = sizes
    col_blocks = density_ref.shape[1] // BLK
    first_row = lax.axis_index("grid") * row_blocks
    first_col = lax.axis_index("col") * col_blocks
    tiles, items = list_tiles(
        sizes, blocks_ref, points_ref, tile_slot, tile_row, tile_col, item_tile, item_half
    )

    def tile_copy(tile):
        row = pl.multiple_of((tile_row[tile] - first_row) * BLK, BLK)
        column = pl.multiple_of((tile_col[tile] - first_col) * BLK, BLK)
        return pltpu.make_async_copy(
            density_ref.at[pl.ds(row, BLK), pl.ds(column, BLK)], held.at[tile], tile_sem.at[tile]
        )

    def fill_copy(index):
        return pltpu.make_async_copy(
            zeros, matrix_ref.at[pl.ds(index * FILL_ROWS, FILL_ROWS), :], fill_sem.at[index]
        )

    @pl.loop(0, tiles)
    def _(tile):
        tile_copy(tile).start()

    zeros[...] = jnp.zeros_like(zeros)
    for index in range(fills):
        fill_copy(index).start()
    sums_ref[...] = jnp.zeros_like(sums_ref)

    @pl.loop(0, tiles)
    def _(tile):
        tile_copy(tile).wait()

    def one(item):
        tile, half = item_tile[item], item_half[item]
        slot = tile_slot[tile]
        points = half_rows(points_ref[slot], half, halves)[0:3]
        rate, centre = functions_of(centres_ref, exponents_ref, tile_row[tile], tile_col[tile])
        value = basis(points, rate, centre)
        low = value.astype(BF16)
        panel = held[tile]
        left_sum = jnp.dot(panel, low[BLK:], preferred_element_type=F32)
        right_sum = lax.dot_general(
            panel, low[:BLK], (((0,), (0,)), ((), ())), preferred_element_type=F32
        )
        product = value * jnp.concatenate([left_sum, right_sum], axis=0)
        summed = jnp.dot(
            coefficients(rate, centre),
            product,
            precision=lax.Precision.HIGHEST,
            preferred_element_type=F32,
        )
        gradient = 2.0 * (summed[1:4] - points * summed[0:1])
        piece = jnp.concatenate([summed[4:5], gradient], axis=0)
        rows = lax.broadcasted_iota(jnp.int32, (4 * halves, BLK), 0)
        return slot, (rows >= 4 * half) & (rows < 4 * half + 4), jnp.concatenate([piece] * halves, 0)

    @pl.loop(0, lax.div(items + 1, 2))
    def _(pair):
        results = [one(2 * pair), one(jnp.minimum(2 * pair + 1, items - 1))]
        for slot, chosen, piece in results:
            sums_ref[slot] = jnp.where(chosen, piece, sums_ref[slot])

    for index in range(fills):
        fill_copy(index).wait()


def potential_tiles(
    sizes,
    fills,
    blocks_ref,
    points_ref,
    fields_ref,
    extra_ref,
    centres_ref,
    exponents_ref,
    given_ref,
    matrix_ref,
    samples_ref,
    amounts_ref,
    total,
    zeros,
    tile_slot,
    tile_row,
    tile_col,
    item_tile,
    item_half,
    tile_goal,
    tile_sem,
    fill_sem,
):
    grid_size, col_size, batches, row_blocks, halves = sizes
    row_count, col_count = matrix_ref.shape
    first_row = lax.axis_index("grid") * row_blocks
    first_col = lax.axis_index("col") * (col_count // BLK)

    def fill_copy(index):
        return pltpu.make_async_copy(
            zeros, matrix_ref.at[pl.ds(index * FILL_ROWS, FILL_ROWS), :], fill_sem.at[index]
        )

    zeros[...] = jnp.zeros_like(zeros)
    every_fill = range(fills, row_count // FILL_ROWS)
    for index in every_fill:
        fill_copy(index).start()
    tiles, items = list_tiles(
        sizes, blocks_ref, points_ref, tile_slot, tile_row, tile_col, item_tile, item_half
    )
    total[...] = jnp.zeros_like(total)

    @pl.loop(0, tiles)
    def _(tile):
        def step(k, goal):
            other = tile - 1 - k
            same = (tile_row[other] == tile_row[tile]) & (tile_col[other] == tile_col[tile])
            return jnp.where(same, other, goal)

        tile_goal[tile] = lax.fori_loop(0, tile, step, tile)

    for batch in range(batches):
        for half in range(halves):
            place = batch * halves + half
            samples_ref[batch : batch + 1, half * BLK : (half + 1) * BLK] = extra_ref[
                0, place : place + 1, :
            ]
        amounts_ref[batch] = jnp.sum(extra_ref[1, batch * halves : (batch + 1) * halves, :])

    def one(item):
        tile, half = item_tile[item], item_half[item]
        slot = tile_slot[tile]
        points = half_rows(points_ref[slot], half, halves)[0:3]
        field = half_rows(fields_ref[slot], half, halves)
        rate, centre = functions_of(centres_ref, exponents_ref, tile_row[tile], tile_col[tile])
        value = basis(points, rate, centre)
        slant = -2.0 * jnp.sum(field[1:4] * points, axis=0, keepdims=True)
        right = jnp.concatenate(
            [slant, 2.0 * field[1:4], field[0:1], jnp.zeros((3, BLK), F32)], axis=0
        )
        weighted = (value * outer_sum(coefficients(rate, centre), right)).astype(BF16)
        low = value.astype(BF16)
        left_side = jnp.concatenate([low[:BLK], weighted[:BLK]], axis=1)
        right_side = jnp.concatenate([weighted[BLK:], low[BLK:]], axis=1)
        return tile, lax.dot_general(
            left_side, right_side, (((1,), (1,)), ((), ())), preferred_element_type=F32
        )

    @pl.loop(0, lax.div(items + 1, 2))
    def _(pair):
        tile_a, result_a = one(2 * pair)
        second = 2 * pair + 1
        tile_b, result_b = one(jnp.minimum(second, items - 1))
        goal_a = tile_goal[tile_a]
        goal_b = jnp.where(second < items, tile_goal[tile_b], grid_size)
        total[goal_a] += result_a
        total[goal_b] += result_b

    for index in every_fill:
        fill_copy(index).wait()

    def tile_copy(tile):
        row = pl.multiple_of((tile_row[tile] - first_row) * BLK, BLK)
        column = pl.multiple_of((tile_col[tile] - first_col) * BLK, BLK)
        return pltpu.make_async_copy(
            total.at[tile], matrix_ref.at[pl.ds(row, BLK), pl.ds(column, BLK)], tile_sem.at[tile]
        )

    @pl.loop(0, tiles)
    def _(tile):
        @pl.when(tile_goal[tile] == tile)
        def _():
            tile_copy(tile).start()

    @pl.loop(0, tiles)
    def _(tile):
        @pl.when(tile_goal[tile] == tile)
        def _():
            tile_copy(tile).wait()


def local(density, centres, exponents, coords, weights, core_density, counts, blocks):
    grid_size = lax.axis_size("grid")
    col_size = lax.axis_size("col")
    row_count, col_count = density.shape
    batches, _, points_len = coords.shape
    row_blocks = row_count // BLK
    halves = points_len // BLK
    sizes = (grid_size, col_size, batches, row_blocks, halves)
    rates = exponents.reshape(exponents.shape[0] // BLK, BLK)
    vmem = pl.BlockSpec(memory_space=pltpu.VMEM)
    smem = pl.BlockSpec(memory_space=pltpu.SMEM)
    anywhere = pl.BlockSpec(memory_space=pl.ANY)
    slot_shape = (grid_size, 4 * halves, BLK)
    slots = jax.ShapeDtypeStruct(slot_shape, F32)
    matrix = jax.ShapeDtypeStruct((row_count, col_count), F32)
    all_fills = row_count // FILL_ROWS
    fills = int(all_fills * FIRST_FILL)

    points = pl.pallas_call(
        lambda *refs: exchange_points(sizes, *refs),
        out_shape=slots,
        in_specs=[smem, smem, vmem],
        out_specs=vmem,
        scratch_shapes=[
            pltpu.VMEM(slot_shape, F32),
            pltpu.VMEM(slot_shape, F32),
            pltpu.SemaphoreType.DMA((grid_size,)),
            pltpu.SemaphoreType.DMA((grid_size,)),
        ],
        compiler_params=pltpu.CompilerParams(
            collective_id=0, has_side_effects=True, vmem_limit_bytes=VMEM_LIMIT
        ),
        name="exchange_points",
    )(blocks, counts, coords)

    lists = [pltpu.SMEM((grid_size + 1,), jnp.int32)] * 3 + [
        pltpu.SMEM((halves * grid_size + 1,), jnp.int32)
    ] * 2
    sums, started = pl.pallas_call(
        lambda *refs: density_tiles(sizes, fills, *refs),
        out_shape=(slots, matrix),
        in_specs=[smem, vmem, anywhere, vmem, vmem],
        out_specs=(vmem, anywhere),
        scratch_shapes=[
            pltpu.VMEM((grid_size, BLK, BLK), BF16),
            pltpu.VMEM((FILL_ROWS, col_count), F32),
            *lists,
            pltpu.SemaphoreType.DMA((grid_size,)),
            pltpu.SemaphoreType.DMA((all_fills,)),
        ],
        compiler_params=pltpu.CompilerParams(vmem_limit_bytes=VMEM_LIMIT),
        name="density_tiles",
    )(blocks, points, density, centres, rates)

    fields, extra = pl.pallas_call(
        lambda *refs: exchange_sums(sizes, *refs),
        out_shape=(slots, jax.ShapeDtypeStruct((2, batches * halves, BLK), F32)),
        in_specs=[smem, smem, vmem, vmem, vmem],
        out_specs=(vmem, vmem),
        scratch_shapes=[
            pltpu.VMEM(slot_shape, F32),
            pltpu.VMEM((col_size, batches, 4 * halves, BLK), F32),
            pltpu.VMEM((batches, 4 * halves, BLK), F32),
            pltpu.VMEM(slot_shape, F32),
            pltpu.VMEM(slot_shape, F32),
            pltpu.SemaphoreType.DMA((grid_size,)),
            pltpu.SemaphoreType.DMA((grid_size,)),
            pltpu.SemaphoreType.DMA((col_size,)),
            pltpu.SemaphoreType.DMA((col_size,)),
            pltpu.SemaphoreType.DMA((grid_size,)),
            pltpu.SemaphoreType.DMA((grid_size,)),
        ],
        compiler_params=pltpu.CompilerParams(
            collective_id=1, has_side_effects=True, vmem_limit_bytes=VMEM_LIMIT
        ),
        name="exchange_sums",
    )(blocks, counts, sums, weights, core_density)

    return pl.pallas_call(
        lambda *refs: potential_tiles(sizes, fills, *refs),
        out_shape=(
            matrix,
            jax.ShapeDtypeStruct((batches, points_len), F32),
            jax.ShapeDtypeStruct((batches,), F32),
        ),
        in_specs=[smem, vmem, vmem, vmem, vmem, vmem, anywhere],
        out_specs=(anywhere, vmem, smem),
        scratch_shapes=[
            pltpu.VMEM((grid_size + 1, BLK, BLK), F32),
            pltpu.VMEM((FILL_ROWS, col_count), F32),
            *lists,
            pltpu.SMEM((grid_size + 1,), jnp.int32),
            pltpu.SemaphoreType.DMA((grid_size,)),
            pltpu.SemaphoreType.DMA((all_fills,)),
        ],
        input_output_aliases={6: 0},
        compiler_params=pltpu.CompilerParams(vmem_limit_bytes=VMEM_LIMIT),
        name="potential_tiles",
    )(blocks, points, fields, extra, centres, rates, started)


def solution(mesh):
    return jax.shard_map(
        local,
        mesh=mesh,
        in_specs=(
            P("grid", "col"),
            P(),
            P(),
            P("grid", None, None),
            P("grid", None),
            P("grid", None),
            P("grid"),
            P(),
        ),
        out_specs=(P("grid", "col"), P("grid", None), P("grid")),
        check_vma=False,
    )
```

```python
import math

import jax
import jax.numpy as jnp
from jax import lax
from jax.experimental import pallas as pl
from jax.experimental.pallas import tpu as pltpu
from jax.sharding import PartitionSpec as P

BLK = 128
FILL_ROWS = 32
FIRST_FILL = 0.5
VMEM_LIMIT = 64 * 1024 * 1024
MESH = pl.DeviceIdType.MESH
F32 = jnp.float32
BF16 = jnp.bfloat16

kappa_pbe = 0.804
mu_coef = 0.2195
slater = -0.7385587663820224
grad_scale = 4.0 * (3.0 * math.pi**2) ** (2.0 / 3.0)
soft_square = 0.25


def xc_kernel(total, grad_square):
    root = jnp.sqrt(total * total + soft_square)
    regular = 0.5 * (total + root)
    log_regular = jnp.log(regular)
    third = jnp.exp(log_regular * (1.0 / 3.0))
    four_thirds = jnp.exp(log_regular * (4.0 / 3.0))
    scaled = grad_scale * four_thirds * four_thirds
    inverse = 1.0 / (kappa_pbe * scaled + mu_coef * grad_square)
    ratio = scaled * inverse
    enhance = 1.0 + kappa_pbe - kappa_pbe * kappa_pbe * ratio
    energy = slater * four_thirds * enhance
    inner = (4.0 / 3.0) * enhance - (8.0 / 3.0) * kappa_pbe * kappa_pbe * ratio * (
        mu_coef * grad_square * inverse
    )
    deriv_density = slater * third * inner * (0.5 * (1.0 + total / root))
    deriv_sigma = slater * four_thirds * (kappa_pbe * kappa_pbe * mu_coef) * ratio * inverse
    return energy, deriv_density, deriv_sigma


def parts_of(value):
    first = value.astype(BF16).astype(F32)
    rest = value - first
    second = rest.astype(BF16).astype(F32)
    return first, second, rest - second


def outer_sum(left, right):
    l1, l2, l3 = parts_of(left)
    r1, r2, r3 = parts_of(right)
    lefts = jnp.concatenate([l1, l1, l1, l2, l2, l3], axis=0).astype(BF16)
    rights = jnp.concatenate([r1, r2, r3, r1, r2, r1], axis=0).astype(BF16)
    return lax.dot_general(
        lefts, rights, (((0,), (0,)), ((), ())), preferred_element_type=F32
    )


def batch_of(blocks_ref, requester, entry, owner, batches, row_blocks):
    found = jnp.int32(-1)
    for batch in range(batches):
        offset = blocks_ref[entry, requester * batches + batch] - owner * row_blocks
        found = jnp.where((offset >= 0) & (offset < row_blocks), batch, found)
    return found


def owners_of(sizes, blocks_ref, requester):
    grid_size, col_size, batches, row_blocks, halves = sizes
    return [
        [lax.div(blocks_ref[entry, requester * batches + batch], row_blocks) for batch in range(batches)]
        for entry in range(col_size)
    ]


def asked_batch(sizes, owners, owner):
    grid_size, col_size, batches, row_blocks, halves = sizes
    found = jnp.int32(0)
    for batch in range(1, batches):
        found = jnp.where(owners[owner // (grid_size // col_size)][batch] == owner, batch, found)
    return found


def fetch(pairs, sems):
    copies = [
        pltpu.make_async_copy(source, target, sems.at[place])
        for place, (source, target) in enumerate(pairs)
    ]
    for copy in copies:
        copy.start()
    return copies


def exchange_points(
    sizes,
    blocks_hbm,
    counts_hbm,
    coords_hbm,
    out_ref,
    blocks_ref,
    counts_ref,
    coords_ref,
    packed,
    staged,
    fetch_sem,
    own_sem,
    send,
    recv,
):
    grid_size, col_size, batches, row_blocks, halves = sizes
    me, col = lax.axis_index("grid"), lax.axis_index("col")
    fetched = fetch(
        [(blocks_hbm, blocks_ref), (counts_hbm, counts_ref), (coords_hbm, coords_ref)], fetch_sem
    )
    barrier = pltpu.get_barrier_semaphore()
    for step in range(1, grid_size):
        other = lax.rem(me + step, grid_size)
        pl.semaphore_signal(barrier, inc=1, device_id=(other, col), device_id_type=MESH)
    for copy in fetched:
        copy.wait()
    points = coords_ref[...]
    for batch in range(batches):
        count = jnp.full((1, BLK), counts_ref[batch].astype(F32), F32)
        pieces = []
        for half in range(halves):
            lanes = slice(half * BLK, (half + 1) * BLK)
            pieces += [points[d, batch : batch + 1, lanes] for d in range(3)] + [count]
        packed[batch] = jnp.concatenate(pieces, axis=0)
    owners = owners_of(sizes, blocks_ref, me)
    for owner in range(grid_size):
        staged[owner] = packed[asked_batch(sizes, owners, owner)]
    pl.semaphore_wait(barrier, grid_size - 1)
    copies = []
    for step in range(1, grid_size):
        other = lax.rem(me + step, grid_size)
        copy = pltpu.make_async_remote_copy(
            src_ref=staged.at[other],
            dst_ref=out_ref.at[me],
            send_sem=send.at[step],
            recv_sem=recv.at[step],
            device_id=(other, col),
            device_id_type=MESH,
        )
        copy.start()
        copies.append(copy)
    own = pltpu.make_async_copy(staged.at[me], out_ref.at[me], own_sem)
    own.start()
    for copy in copies:
        copy.wait()
    own.wait()


def exchange_sums(
    sizes,
    blocks_hbm,
    counts_hbm,
    weights_hbm,
    core_hbm,
    sums_ref,
    out_ref,
    extra_ref,
    blocks_ref,
    counts_ref,
    weights_ref,
    core_ref,
    fetch_sem,
    landed,
    col_sums,
    fields,
    staged,
    extra,
    own_sem,
    send_a,
    recv_a,
    send_b,
    recv_b,
    send_c,
    recv_c,
):
    grid_size, col_size, batches, row_blocks, halves = sizes
    me, col = lax.axis_index("grid"), lax.axis_index("col")
    fetched = fetch(
        [
            (blocks_hbm, blocks_ref),
            (counts_hbm, counts_ref),
            (weights_hbm, weights_ref),
            (core_hbm, core_ref),
        ],
        fetch_sem,
    )
    barrier = pltpu.get_barrier_semaphore()
    for step in range(1, grid_size):
        other = lax.rem(me + step, grid_size)
        pl.semaphore_signal(barrier, inc=1, device_id=(other, col), device_id_type=MESH)
    for step in range(1, col_size):
        other = lax.rem(col + step, col_size)
        pl.semaphore_signal(barrier, inc=1, device_id=(me, other), device_id_type=MESH)
    for copy in fetched:
        copy.wait()
    owners = owners_of(sizes, blocks_ref, me)
    asked = [asked_batch(sizes, owners, owner) for owner in range(grid_size)]
    pl.semaphore_wait(barrier, grid_size + col_size - 2)

    copies = []
    for step in range(1, grid_size):
        other = lax.rem(me + step, grid_size)
        copy = pltpu.make_async_remote_copy(
            src_ref=sums_ref.at[other],
            dst_ref=landed.at[me],
            send_sem=send_a.at[step],
            recv_sem=recv_a.at[step],
            device_id=(other, col),
            device_id_type=MESH,
        )
        copy.start()
        copies.append(copy)
    kept = fetch([(sums_ref.at[me], landed.at[me])], own_sem)
    for copy in copies:
        copy.wait()
    kept[0].wait()

    for batch in range(batches):
        total = None
        for entry in range(col_size):
            term = landed[owners[entry][batch]]
            total = term if total is None else total + term
        col_sums[col, batch] = total
    copies = []
    for step in range(1, col_size):
        other = lax.rem(col + step, col_size)
        copy = pltpu.make_async_remote_copy(
            src_ref=col_sums.at[col],
            dst_ref=col_sums.at[col],
            send_sem=send_b.at[step],
            recv_sem=recv_b.at[step],
            device_id=(me, other),
            device_id_type=MESH,
        )
        copy.start()
        copies.append(copy)
    for copy in copies:
        copy.wait()
    summed = col_sums[0]
    for entry in range(1, col_size):
        summed = summed + col_sums[entry]

    places = [(batch, half) for batch in range(batches) for half in range(halves)]

    def rows_of(field):
        return jnp.concatenate(
            [summed[batch, 4 * half + field : 4 * half + field + 1] for batch, half in places],
            axis=0,
        )

    def rows_in(ref):
        value = ref[...]
        return jnp.concatenate(
            [value[batch : batch + 1, half * BLK : (half + 1) * BLK] for batch, half in places],
            axis=0,
        )

    lanes = lax.broadcasted_iota(jnp.int32, (1, BLK), 1)
    live = jnp.concatenate(
        [jnp.where(lanes + half * BLK < counts_ref[batch], 1.0, 0.0) for batch, half in places],
        axis=0,
    )
    valence = jnp.where(live > 0.0, rows_of(0), 0.0)
    gradient = [jnp.where(live > 0.0, rows_of(1 + d), 0.0) for d in range(3)]
    grad_square = (
        gradient[0] * gradient[0] + gradient[1] * gradient[1] + gradient[2] * gradient[2]
    )
    energy, deriv_density, deriv_sigma = xc_kernel(valence + rows_in(core_ref), grad_square)
    point_scale = rows_in(weights_ref) * live
    spread = 2.0 * point_scale * deriv_sigma
    table = [point_scale * deriv_density] + [spread * gradient[d] for d in range(3)]
    for batch in range(batches):
        fields[batch] = jnp.concatenate(
            [
                table[k][batch * halves + half : batch * halves + half + 1]
                for half in range(halves)
                for k in range(4)
            ],
            axis=0,
        )
    for owner in range(grid_size):
        staged[owner] = fields[asked[owner]]
    copies = []
    for step in range(1, grid_size):
        other = lax.rem(me + step, grid_size)
        copy = pltpu.make_async_remote_copy(
            src_ref=staged.at[other],
            dst_ref=out_ref.at[me],
            send_sem=send_c.at[step],
            recv_sem=recv_c.at[step],
            device_id=(other, col),
            device_id_type=MESH,
        )
        copy.start()
        copies.append(copy)
    extra[0] = valence
    extra[1] = point_scale * energy
    kept = fetch([(staged.at[me], out_ref.at[me]), (extra, extra_ref)], own_sem)
    for copy in copies:
        copy.wait()
    for copy in kept:
        copy.wait()


def list_tiles(sizes, blocks_ref, points_ref, tile_slot, tile_row, tile_col, item_tile, item_half):
    grid_size, col_size, batches, row_blocks, halves = sizes
    me, col = lax.axis_index("grid"), lax.axis_index("col")
    entry = lax.div(me, grid_size // col_size)

    def step(slot, carry):
        tiles, items = carry
        found = batch_of(blocks_ref, slot, entry, me, batches, row_blocks)
        batch = jnp.maximum(found, 0)
        has = found >= 0
        tile_slot[tiles] = slot
        tile_row[tiles] = blocks_ref[entry, slot * batches + batch]
        tile_col[tiles] = blocks_ref[col, slot * batches + batch]
        count = points_ref[slot, 3, 0]
        for half in range(halves):
            item_tile[items] = tiles
            item_half[items] = half
            items = items + jnp.where(has & (count > half * BLK), 1, 0)
        return tiles + jnp.where(has, 1, 0), items

    return lax.fori_loop(0, grid_size, step, (jnp.int32(0), jnp.int32(0)))


def half_rows(value, half, halves):
    picked = value[0:4]
    for other in range(1, halves):
        picked = jnp.where(half == other, value[4 * other : 4 * other + 4], picked)
    return picked


def functions_of(centres_ref, exponents_ref, row, column):
    rate = jnp.concatenate(
        [exponents_ref[pl.ds(row, 1), :], exponents_ref[pl.ds(column, 1), :]], axis=1
    )
    centre = jnp.concatenate(
        [
            centres_ref[:, pl.ds(pl.multiple_of(row * BLK, BLK), BLK)],
            centres_ref[:, pl.ds(pl.multiple_of(column * BLK, BLK), BLK)],
        ],
        axis=1,
    )
    return rate, centre


def distance_factors(points, rate, centre):
    square = jnp.sum(points * points, axis=0, keepdims=True)
    right = jnp.concatenate(
        [square, points, jnp.ones((1, BLK), F32), jnp.zeros((3, BLK), F32)], axis=0
    )
    left = jnp.concatenate(
        [
            -rate,
            2.0 * rate * centre,
            -rate * jnp.sum(centre * centre, axis=0, keepdims=True),
            jnp.zeros((3, 2 * BLK), F32),
        ],
        axis=0,
    )
    return right, left


def coefficients(rate, centre):
    lanes = lax.broadcasted_iota(jnp.int32, (1, 2 * BLK), 1)
    return jnp.concatenate(
        [
            rate,
            rate * centre,
            jnp.where(lanes >= BLK, 1.0, 0.0),
            jnp.zeros((3, 2 * BLK), F32),
        ],
        axis=0,
    )


def density_tiles(
    sizes,
    fills,
    blocks_hbm,
    density_ref,
    centres_hbm,
    exponents_hbm,
    points_hbm,
    sums_ref,
    matrix_ref,
    points_ref,
    blocks_ref,
    centres_ref,
    exponents_ref,
    fetch_sem,
    held,
    zeros,
    tile_slot,
    tile_row,
    tile_col,
    item_tile,
    item_half,
    tile_sem,
    fill_sem,
):
    grid_size, col_size, batches, row_blocks, halves = sizes
    col_blocks = density_ref.shape[1] // BLK
    first_row = lax.axis_index("grid") * row_blocks
    first_col = lax.axis_index("col") * col_blocks

    def tile_copy(tile):
        row = pl.multiple_of((tile_row[tile] - first_row) * BLK, BLK)
        column = pl.multiple_of((tile_col[tile] - first_col) * BLK, BLK)
        return pltpu.make_async_copy(
            density_ref.at[pl.ds(row, BLK), pl.ds(column, BLK)], held.at[tile], tile_sem.at[tile]
        )

    def fill_copy(index):
        return pltpu.make_async_copy(
            zeros, matrix_ref.at[pl.ds(index * FILL_ROWS, FILL_ROWS), :], fill_sem.at[index]
        )

    fetched = fetch(
        [
            (blocks_hbm, blocks_ref),
            (points_hbm, points_ref),
            (centres_hbm, centres_ref),
            (exponents_hbm, exponents_ref),
        ],
        fetch_sem,
    )
    zeros[...] = jnp.zeros_like(zeros)
    for index in range(fills):
        fill_copy(index).start()
    sums_ref[...] = jnp.zeros_like(sums_ref)
    fetched[0].wait()
    fetched[1].wait()
    tiles, items = list_tiles(
        sizes, blocks_ref, points_ref, tile_slot, tile_row, tile_col, item_tile, item_half
    )

    @pl.loop(0, tiles)
    def _(tile):
        tile_copy(tile).start()

    fetched[2].wait()
    fetched[3].wait()

    @pl.loop(0, tiles)
    def _(tile):
        tile_copy(tile).wait()

    def one(item):
        tile, half = item_tile[item], item_half[item]
        slot = tile_slot[tile]
        points = half_rows(points_ref[slot], half, halves)[0:3]
        rate, centre = functions_of(centres_ref, exponents_ref, tile_row[tile], tile_col[tile])
        right, left = distance_factors(points, rate, centre)
        value = jnp.exp(outer_sum(right, left))
        low = value.astype(BF16)
        panel = held[tile]
        left_sum = lax.dot_general(
            low[:, BLK:], panel, (((1,), (1,)), ((), ())), preferred_element_type=F32
        )
        right_sum = jnp.dot(low[:, :BLK], panel, preferred_element_type=F32)
        product = value * jnp.concatenate([left_sum, right_sum], axis=1)
        upper = product.astype(BF16)
        lower = (product - upper.astype(F32)).astype(BF16)
        c1, c2, c3 = parts_of(coefficients(rate, centre))
        weights = jnp.concatenate([c1, c2, c3, jnp.zeros((BLK - 24, 2 * BLK), F32)], axis=0)
        weights = weights.astype(BF16)
        contract = (((1,), (1,)), ((), ()))
        first = lax.dot_general(upper, weights, contract, preferred_element_type=F32).T
        second = lax.dot_general(lower, weights, contract, preferred_element_type=F32).T
        summed = first[0:8] + (first[8:16] + second[0:8]) + (first[16:24] + second[8:16])
        gradient = 2.0 * (summed[1:4] - points * summed[0:1])
        piece = jnp.concatenate([summed[4:5], gradient], axis=0)
        rows = lax.broadcasted_iota(jnp.int32, (4 * halves, BLK), 0)
        return slot, (rows >= 4 * half) & (rows < 4 * half + 4), jnp.concatenate([piece] * halves, 0)

    @pl.loop(0, lax.div(items + 1, 2))
    def _(pair):
        results = [one(2 * pair), one(jnp.minimum(2 * pair + 1, items - 1))]
        for slot, chosen, piece in results:
            sums_ref[slot] = jnp.where(chosen, piece, sums_ref[slot])

    for index in range(fills):
        fill_copy(index).wait()


def potential_tiles(
    sizes,
    fills,
    blocks_hbm,
    centres_hbm,
    exponents_hbm,
    points_hbm,
    fields_hbm,
    extra_hbm,
    given_ref,
    matrix_ref,
    samples_ref,
    amounts_ref,
    fields_ref,
    extra_ref,
    points_ref,
    blocks_ref,
    centres_ref,
    exponents_ref,
    fetch_sem,
    total,
    zeros,
    tile_slot,
    tile_row,
    tile_col,
    item_tile,
    item_half,
    tile_goal,
    tile_sem,
    fill_sem,
):
    grid_size, col_size, batches, row_blocks, halves = sizes
    row_count, col_count = matrix_ref.shape
    first_row = lax.axis_index("grid") * row_blocks
    first_col = lax.axis_index("col") * (col_count // BLK)

    def fill_copy(index):
        return pltpu.make_async_copy(
            zeros, matrix_ref.at[pl.ds(index * FILL_ROWS, FILL_ROWS), :], fill_sem.at[index]
        )

    fetched = fetch(
        [
            (blocks_hbm, blocks_ref),
            (points_hbm, points_ref),
            (centres_hbm, centres_ref),
            (exponents_hbm, exponents_ref),
            (fields_hbm, fields_ref),
            (extra_hbm, extra_ref),
        ],
        fetch_sem,
    )
    zeros[...] = jnp.zeros_like(zeros)
    every_fill = range(fills, row_count // FILL_ROWS)
    for index in every_fill:
        fill_copy(index).start()
    fetched[0].wait()
    fetched[1].wait()
    tiles, items = list_tiles(
        sizes, blocks_ref, points_ref, tile_slot, tile_row, tile_col, item_tile, item_half
    )
    total[...] = jnp.zeros_like(total)
    for copy in fetched[2:]:
        copy.wait()

    @pl.loop(0, tiles)
    def _(tile):
        def step(k, goal):
            other = tile - 1 - k
            same = (tile_row[other] == tile_row[tile]) & (tile_col[other] == tile_col[tile])
            return jnp.where(same, other, goal)

        tile_goal[tile] = lax.fori_loop(0, tile, step, tile)

    for batch in range(batches):
        for half in range(halves):
            place = batch * halves + half
            samples_ref[batch : batch + 1, half * BLK : (half + 1) * BLK] = extra_ref[
                0, place : place + 1, :
            ]
        amounts_ref[batch] = jnp.sum(extra_ref[1, batch * halves : (batch + 1) * halves, :])

    def one(item):
        tile, half = item_tile[item], item_half[item]
        slot = tile_slot[tile]
        points = half_rows(points_ref[slot], half, halves)[0:3]
        field = half_rows(fields_ref[slot], half, halves)
        rate, centre = functions_of(centres_ref, exponents_ref, tile_row[tile], tile_col[tile])
        distance_right, distance_left = distance_factors(points, rate, centre)
        value = jnp.exp(outer_sum(distance_left, distance_right))
        slant = -2.0 * jnp.sum(field[1:4] * points, axis=0, keepdims=True)
        right = jnp.concatenate(
            [slant, 2.0 * field[1:4], field[0:1], jnp.zeros((3, BLK), F32)], axis=0
        )
        weighted = (value * outer_sum(coefficients(rate, centre), right)).astype(BF16)
        low = value.astype(BF16)
        left_side = jnp.concatenate([low[:BLK], weighted[:BLK]], axis=1)
        right_side = jnp.concatenate([weighted[BLK:], low[BLK:]], axis=1)
        return tile, lax.dot_general(
            left_side, right_side, (((1,), (1,)), ((), ())), preferred_element_type=F32
        )

    @pl.loop(0, lax.div(items + 1, 2))
    def _(pair):
        tile_a, result_a = one(2 * pair)
        second = 2 * pair + 1
        tile_b, result_b = one(jnp.minimum(second, items - 1))
        goal_a = tile_goal[tile_a]
        goal_b = jnp.where(second < items, tile_goal[tile_b], grid_size)
        total[goal_a] += result_a
        total[goal_b] += result_b

    for index in every_fill:
        fill_copy(index).wait()

    def tile_copy(tile):
        row = pl.multiple_of((tile_row[tile] - first_row) * BLK, BLK)
        column = pl.multiple_of((tile_col[tile] - first_col) * BLK, BLK)
        return pltpu.make_async_copy(
            total.at[tile], matrix_ref.at[pl.ds(row, BLK), pl.ds(column, BLK)], tile_sem.at[tile]
        )

    @pl.loop(0, tiles)
    def _(tile):
        @pl.when(tile_goal[tile] == tile)
        def _():
            tile_copy(tile).start()

    @pl.loop(0, tiles)
    def _(tile):
        @pl.when(tile_goal[tile] == tile)
        def _():
            tile_copy(tile).wait()


def local(density, centres, exponents, coords, weights, core_density, counts, blocks):
    grid_size = lax.axis_size("grid")
    col_size = lax.axis_size("col")
    row_count, col_count = density.shape
    batches, _, points_len = coords.shape
    row_blocks = row_count // BLK
    halves = points_len // BLK
    sizes = (grid_size, col_size, batches, row_blocks, halves)
    rates = exponents.reshape(exponents.shape[0] // BLK, BLK)
    table = blocks.T
    parts_first = coords.transpose(1, 0, 2)
    vmem = pl.BlockSpec(memory_space=pltpu.VMEM)
    smem = pl.BlockSpec(memory_space=pltpu.SMEM)
    anywhere = pl.BlockSpec(memory_space=pl.ANY)
    slot_shape = (grid_size, 4 * halves, BLK)
    hbm = pl.BlockSpec(memory_space=pltpu.HBM)
    table_memory = pltpu.SMEM(table.shape, jnp.int32)
    count_memory = pltpu.SMEM((batches,), jnp.int32)
    function_memory = [
        pltpu.VMEM(slot_shape, F32),
        table_memory,
        pltpu.VMEM(centres.shape, F32),
        pltpu.VMEM(rates.shape, F32),
        pltpu.SemaphoreType.DMA((6,)),
    ]
    slots = jax.ShapeDtypeStruct(slot_shape, F32)
    matrix = jax.ShapeDtypeStruct((row_count, col_count), F32)
    all_fills = row_count // FILL_ROWS
    fills = int(all_fills * FIRST_FILL)

    points = pl.pallas_call(
        lambda *refs: exchange_points(sizes, *refs),
        out_shape=slots,
        in_specs=[hbm, hbm, hbm],
        out_specs=anywhere,
        scratch_shapes=[
            table_memory,
            count_memory,
            pltpu.VMEM(parts_first.shape, F32),
            pltpu.VMEM((batches, 4 * halves, BLK), F32),
            pltpu.VMEM(slot_shape, F32),
            pltpu.SemaphoreType.DMA((3,)),
            pltpu.SemaphoreType.DMA,
            pltpu.SemaphoreType.DMA((grid_size,)),
            pltpu.SemaphoreType.DMA((grid_size,)),
        ],
        compiler_params=pltpu.CompilerParams(
            collective_id=0, has_side_effects=True, vmem_limit_bytes=VMEM_LIMIT
        ),
        name="exchange_points",
    )(table, counts, parts_first)

    lists = [pltpu.SMEM((grid_size + 1,), jnp.int32)] * 3 + [
        pltpu.SMEM((halves * grid_size + 1,), jnp.int32)
    ] * 2
    sums, started = pl.pallas_call(
        lambda *refs: density_tiles(sizes, fills, *refs),
        out_shape=(slots, matrix),
        in_specs=[hbm] * 5,
        out_specs=(vmem, anywhere),
        scratch_shapes=[
            *function_memory,
            pltpu.VMEM((grid_size, BLK, BLK), BF16),
            pltpu.VMEM((FILL_ROWS, col_count), F32),
            *lists,
            pltpu.SemaphoreType.DMA((grid_size,)),
            pltpu.SemaphoreType.DMA((all_fills,)),
        ],
        compiler_params=pltpu.CompilerParams(vmem_limit_bytes=VMEM_LIMIT),
        name="density_tiles",
    )(table, density, centres, rates, points)

    fields, extra = pl.pallas_call(
        lambda *refs: exchange_sums(sizes, *refs),
        out_shape=(slots, jax.ShapeDtypeStruct((2, batches * halves, BLK), F32)),
        in_specs=[hbm, hbm, hbm, hbm, hbm],
        out_specs=(anywhere, anywhere),
        scratch_shapes=[
            table_memory,
            count_memory,
            pltpu.VMEM(weights.shape, F32),
            pltpu.VMEM(core_density.shape, F32),
            pltpu.SemaphoreType.DMA((4,)),
            pltpu.VMEM(slot_shape, F32),
            pltpu.VMEM((col_size, batches, 4 * halves, BLK), F32),
            pltpu.VMEM((batches, 4 * halves, BLK), F32),
            pltpu.VMEM(slot_shape, F32),
            pltpu.VMEM((2, batches * halves, BLK), F32),
            pltpu.SemaphoreType.DMA((2,)),
            pltpu.SemaphoreType.DMA((grid_size,)),
            pltpu.SemaphoreType.DMA((grid_size,)),
            pltpu.SemaphoreType.DMA((col_size,)),
            pltpu.SemaphoreType.DMA((col_size,)),
            pltpu.SemaphoreType.DMA((grid_size,)),
            pltpu.SemaphoreType.DMA((grid_size,)),
        ],
        compiler_params=pltpu.CompilerParams(
            collective_id=1, has_side_effects=True, vmem_limit_bytes=VMEM_LIMIT
        ),
        name="exchange_sums",
    )(table, counts, weights, core_density, sums)

    return pl.pallas_call(
        lambda *refs: potential_tiles(sizes, fills, *refs),
        out_shape=(
            matrix,
            jax.ShapeDtypeStruct((batches, points_len), F32),
            jax.ShapeDtypeStruct((batches,), F32),
        ),
        in_specs=[hbm] * 6 + [anywhere],
        out_specs=(anywhere, vmem, smem),
        scratch_shapes=[
            pltpu.VMEM(slot_shape, F32),
            pltpu.VMEM((2, batches * halves, BLK), F32),
            *function_memory,
            pltpu.VMEM((grid_size + 1, BLK, BLK), F32),
            pltpu.VMEM((FILL_ROWS, col_count), F32),
            *lists,
            pltpu.SMEM((grid_size + 1,), jnp.int32),
            pltpu.SemaphoreType.DMA((grid_size,)),
            pltpu.SemaphoreType.DMA((all_fills,)),
        ],
        input_output_aliases={6: 0},
        compiler_params=pltpu.CompilerParams(vmem_limit_bytes=VMEM_LIMIT),
        name="potential_tiles",
    )(table, centres, rates, points, fields, extra, started)


def solution(mesh):
    return jax.shard_map(
        local,
        mesh=mesh,
        in_specs=(
            P("grid", "col"),
            P(),
            P(),
            P("grid", None, None),
            P("grid", None),
            P("grid", None),
            P("grid"),
            P(),
        ),
        out_specs=(P("grid", "col"), P("grid", None), P("grid")),
        check_vma=False,
    )
```

```python
import math

import jax
import jax.numpy as jnp
from jax import lax
from jax.experimental import pallas as pl
from jax.experimental.pallas import tpu as pltpu
from jax.sharding import PartitionSpec as P

BLK = 128
FILL_ROWS = 32
FIRST_FILL = 0.5
GROUP = 4
VMEM_LIMIT = 64 * 1024 * 1024
MESH = pl.DeviceIdType.MESH
F32 = jnp.float32
BF16 = jnp.bfloat16

kappa_pbe = 0.804
mu_coef = 0.2195
slater = -0.7385587663820224
grad_scale = 4.0 * (3.0 * math.pi**2) ** (2.0 / 3.0)
soft_square = 0.25


def xc_kernel(total, grad_square):
    root = jnp.sqrt(total * total + soft_square)
    regular = 0.5 * (total + root)
    log_regular = jnp.log(regular)
    third = jnp.exp(log_regular * (1.0 / 3.0))
    four_thirds = jnp.exp(log_regular * (4.0 / 3.0))
    scaled = grad_scale * four_thirds * four_thirds
    inverse = 1.0 / (kappa_pbe * scaled + mu_coef * grad_square)
    ratio = scaled * inverse
    enhance = 1.0 + kappa_pbe - kappa_pbe * kappa_pbe * ratio
    energy = slater * four_thirds * enhance
    inner = (4.0 / 3.0) * enhance - (8.0 / 3.0) * kappa_pbe * kappa_pbe * ratio * (
        mu_coef * grad_square * inverse
    )
    deriv_density = slater * third * inner * (0.5 * (1.0 + total / root))
    deriv_sigma = slater * four_thirds * (kappa_pbe * kappa_pbe * mu_coef) * ratio * inverse
    return energy, deriv_density, deriv_sigma


def parts_of(value):
    first = value.astype(BF16).astype(F32)
    rest = value - first
    second = rest.astype(BF16).astype(F32)
    return first, second, rest - second


def outer_sum(left, right):
    l1, l2, l3 = parts_of(left)
    r1, r2, r3 = parts_of(right)
    lefts = jnp.concatenate([l1, l1, l1, l2, l2, l3], axis=0).astype(BF16)
    rights = jnp.concatenate([r1, r2, r3, r1, r2, r1], axis=0).astype(BF16)
    return lax.dot_general(
        lefts, rights, (((0,), (0,)), ((), ())), preferred_element_type=F32
    )


def batch_of(blocks_ref, requester, entry, owner, batches, row_blocks):
    found = jnp.int32(-1)
    for batch in range(batches):
        offset = blocks_ref[entry, requester * batches + batch] - owner * row_blocks
        found = jnp.where((offset >= 0) & (offset < row_blocks), batch, found)
    return found


def owners_of(sizes, blocks_ref, requester):
    grid_size, col_size, batches, row_blocks, halves = sizes
    return [
        [lax.div(blocks_ref[entry, requester * batches + batch], row_blocks) for batch in range(batches)]
        for entry in range(col_size)
    ]


def asked_batch(sizes, owners, owner):
    grid_size, col_size, batches, row_blocks, halves = sizes
    found = jnp.int32(0)
    for batch in range(1, batches):
        found = jnp.where(owners[owner // (grid_size // col_size)][batch] == owner, batch, found)
    return found


def fetch(pairs, sems):
    copies = [
        pltpu.make_async_copy(source, target, sems.at[place])
        for place, (source, target) in enumerate(pairs)
    ]
    for copy in copies:
        copy.start()
    return copies


def exchange_points(
    sizes,
    blocks_hbm,
    counts_hbm,
    coords_hbm,
    out_ref,
    blocks_ref,
    counts_ref,
    coords_ref,
    packed,
    staged,
    fetch_sem,
    own_sem,
    send,
    recv,
):
    grid_size, col_size, batches, row_blocks, halves = sizes
    me, col = lax.axis_index("grid"), lax.axis_index("col")
    fetched = fetch(
        [(blocks_hbm, blocks_ref), (counts_hbm, counts_ref), (coords_hbm, coords_ref)], fetch_sem
    )
    barrier = pltpu.get_barrier_semaphore()
    for step in range(1, grid_size):
        other = lax.rem(me + step, grid_size)
        pl.semaphore_signal(barrier, inc=1, device_id=(other, col), device_id_type=MESH)
    for copy in fetched:
        copy.wait()
    points = coords_ref[...]
    for batch in range(batches):
        count = jnp.full((1, BLK), counts_ref[batch].astype(F32), F32)
        pieces = []
        for half in range(halves):
            lanes = slice(half * BLK, (half + 1) * BLK)
            pieces += [points[d, batch : batch + 1, lanes] for d in range(3)] + [count]
        packed[batch] = jnp.concatenate(pieces, axis=0)
    owners = owners_of(sizes, blocks_ref, me)
    for owner in range(grid_size):
        staged[owner] = packed[asked_batch(sizes, owners, owner)]
    pl.semaphore_wait(barrier, grid_size - 1)
    copies = []
    for step in range(1, grid_size):
        other = lax.rem(me + step, grid_size)
        copy = pltpu.make_async_remote_copy(
            src_ref=staged.at[other],
            dst_ref=out_ref.at[me],
            send_sem=send.at[step],
            recv_sem=recv.at[step],
            device_id=(other, col),
            device_id_type=MESH,
        )
        copy.start()
        copies.append(copy)
    own = pltpu.make_async_copy(staged.at[me], out_ref.at[me], own_sem)
    own.start()
    for copy in copies:
        copy.wait()
    own.wait()


def exchange_sums(
    sizes,
    blocks_hbm,
    counts_hbm,
    weights_hbm,
    core_hbm,
    sums_hbm,
    out_ref,
    extra_ref,
    sums_ref,
    blocks_ref,
    counts_ref,
    weights_ref,
    core_ref,
    fetch_sem,
    landed,
    col_sums,
    fields,
    staged,
    extra,
    own_sem,
    send_a,
    recv_a,
    send_b,
    recv_b,
    send_c,
    recv_c,
):
    grid_size, col_size, batches, row_blocks, halves = sizes
    me, col = lax.axis_index("grid"), lax.axis_index("col")
    fetched = fetch(
        [
            (blocks_hbm, blocks_ref),
            (counts_hbm, counts_ref),
            (weights_hbm, weights_ref),
            (core_hbm, core_ref),
            (sums_hbm, sums_ref),
        ],
        fetch_sem,
    )
    barrier = pltpu.get_barrier_semaphore()
    for step in range(1, grid_size):
        other = lax.rem(me + step, grid_size)
        pl.semaphore_signal(barrier, inc=1, device_id=(other, col), device_id_type=MESH)
    for step in range(1, col_size):
        other = lax.rem(col + step, col_size)
        pl.semaphore_signal(barrier, inc=1, device_id=(me, other), device_id_type=MESH)
    for copy in fetched:
        copy.wait()
    owners = owners_of(sizes, blocks_ref, me)
    asked = [asked_batch(sizes, owners, owner) for owner in range(grid_size)]
    pl.semaphore_wait(barrier, grid_size + col_size - 2)

    copies = []
    for step in range(1, grid_size):
        other = lax.rem(me + step, grid_size)
        copy = pltpu.make_async_remote_copy(
            src_ref=sums_ref.at[other],
            dst_ref=landed.at[me],
            send_sem=send_a.at[step],
            recv_sem=recv_a.at[step],
            device_id=(other, col),
            device_id_type=MESH,
        )
        copy.start()
        copies.append(copy)
    kept = fetch([(sums_ref.at[me], landed.at[me])], own_sem)
    for copy in copies:
        copy.wait()
    kept[0].wait()

    for batch in range(batches):
        total = None
        for entry in range(col_size):
            term = landed[owners[entry][batch]]
            total = term if total is None else total + term
        col_sums[col, batch] = total
    copies = []
    for step in range(1, col_size):
        other = lax.rem(col + step, col_size)
        copy = pltpu.make_async_remote_copy(
            src_ref=col_sums.at[col],
            dst_ref=col_sums.at[col],
            send_sem=send_b.at[step],
            recv_sem=recv_b.at[step],
            device_id=(me, other),
            device_id_type=MESH,
        )
        copy.start()
        copies.append(copy)
    for copy in copies:
        copy.wait()
    summed = col_sums[0]
    for entry in range(1, col_size):
        summed = summed + col_sums[entry]

    places = [(batch, half) for batch in range(batches) for half in range(halves)]

    def rows_of(field):
        return jnp.concatenate(
            [summed[batch, 4 * half + field : 4 * half + field + 1] for batch, half in places],
            axis=0,
        )

    def rows_in(ref):
        value = ref[...]
        return jnp.concatenate(
            [value[batch : batch + 1, half * BLK : (half + 1) * BLK] for batch, half in places],
            axis=0,
        )

    lanes = lax.broadcasted_iota(jnp.int32, (1, BLK), 1)
    live = jnp.concatenate(
        [jnp.where(lanes + half * BLK < counts_ref[batch], 1.0, 0.0) for batch, half in places],
        axis=0,
    )
    valence = jnp.where(live > 0.0, rows_of(0), 0.0)
    gradient = [jnp.where(live > 0.0, rows_of(1 + d), 0.0) for d in range(3)]
    grad_square = (
        gradient[0] * gradient[0] + gradient[1] * gradient[1] + gradient[2] * gradient[2]
    )
    energy, deriv_density, deriv_sigma = xc_kernel(valence + rows_in(core_ref), grad_square)
    point_scale = rows_in(weights_ref) * live
    spread = 2.0 * point_scale * deriv_sigma
    table = [point_scale * deriv_density] + [spread * gradient[d] for d in range(3)]
    for batch in range(batches):
        fields[batch] = jnp.concatenate(
            [
                table[k][batch * halves + half : batch * halves + half + 1]
                for half in range(halves)
                for k in range(4)
            ],
            axis=0,
        )
    for owner in range(grid_size):
        staged[owner] = fields[asked[owner]]
    copies = []
    for step in range(1, grid_size):
        other = lax.rem(me + step, grid_size)
        copy = pltpu.make_async_remote_copy(
            src_ref=staged.at[other],
            dst_ref=out_ref.at[me],
            send_sem=send_c.at[step],
            recv_sem=recv_c.at[step],
            device_id=(other, col),
            device_id_type=MESH,
        )
        copy.start()
        copies.append(copy)
    extra[0] = valence
    extra[1] = point_scale * energy
    kept = fetch([(staged.at[me], out_ref.at[me]), (extra, extra_ref)], own_sem)
    for copy in copies:
        copy.wait()
    for copy in kept:
        copy.wait()


def list_tiles(sizes, blocks_ref, points_ref, tile_slot, tile_row, tile_col, item_tile, item_half):
    grid_size, col_size, batches, row_blocks, halves = sizes
    me, col = lax.axis_index("grid"), lax.axis_index("col")
    entry = lax.div(me, grid_size // col_size)

    def step(slot, carry):
        tiles, items = carry
        found = batch_of(blocks_ref, slot, entry, me, batches, row_blocks)
        batch = jnp.maximum(found, 0)
        has = found >= 0
        tile_slot[tiles] = slot
        tile_row[tiles] = blocks_ref[entry, slot * batches + batch]
        tile_col[tiles] = blocks_ref[col, slot * batches + batch]
        count = points_ref[slot, 3, 0]
        for half in range(halves):
            item_tile[items] = tiles
            item_half[items] = half
            items = items + jnp.where(has & (count > half * BLK), 1, 0)
        return tiles + jnp.where(has, 1, 0), items

    return lax.fori_loop(0, grid_size, step, (jnp.int32(0), jnp.int32(0)), unroll=True)


def half_rows(value, half, halves):
    picked = value[0:4]
    for other in range(1, halves):
        picked = jnp.where(half == other, value[4 * other : 4 * other + 4], picked)
    return picked


def functions_of(centres_ref, exponents_ref, row, column):
    rate = jnp.concatenate(
        [exponents_ref[pl.ds(row, 1), :], exponents_ref[pl.ds(column, 1), :]], axis=1
    )
    centre = jnp.concatenate(
        [
            centres_ref[:, pl.ds(pl.multiple_of(row * BLK, BLK), BLK)],
            centres_ref[:, pl.ds(pl.multiple_of(column * BLK, BLK), BLK)],
        ],
        axis=1,
    )
    return rate, centre


def distance_factors(points, rate, centre):
    square = jnp.sum(points * points, axis=0, keepdims=True)
    right = jnp.concatenate(
        [square, points, jnp.ones((1, BLK), F32), jnp.zeros((3, BLK), F32)], axis=0
    )
    left = jnp.concatenate(
        [
            -rate,
            2.0 * rate * centre,
            -rate * jnp.sum(centre * centre, axis=0, keepdims=True),
            jnp.zeros((3, 2 * BLK), F32),
        ],
        axis=0,
    )
    return right, left


def coefficients(rate, centre):
    lanes = lax.broadcasted_iota(jnp.int32, (1, 2 * BLK), 1)
    return jnp.concatenate(
        [
            rate,
            rate * centre,
            jnp.where(lanes >= BLK, 1.0, 0.0),
            jnp.zeros((3, 2 * BLK), F32),
        ],
        axis=0,
    )


def density_tiles(
    sizes,
    fills,
    blocks_hbm,
    density_ref,
    centres_hbm,
    exponents_hbm,
    points_hbm,
    sums_ref,
    matrix_ref,
    points_ref,
    blocks_ref,
    centres_ref,
    exponents_ref,
    fetch_sem,
    held,
    zeros,
    tile_slot,
    tile_row,
    tile_col,
    item_tile,
    item_half,
    tile_sem,
    fill_sem,
):
    grid_size, col_size, batches, row_blocks, halves = sizes
    col_blocks = density_ref.shape[1] // BLK
    first_row = lax.axis_index("grid") * row_blocks
    first_col = lax.axis_index("col") * col_blocks

    def tile_copy(tile):
        row = pl.multiple_of((tile_row[tile] - first_row) * BLK, BLK)
        column = pl.multiple_of((tile_col[tile] - first_col) * BLK, BLK)
        return pltpu.make_async_copy(
            density_ref.at[pl.ds(row, BLK), pl.ds(column, BLK)], held.at[tile], tile_sem.at[tile]
        )

    def fill_copy(index):
        return pltpu.make_async_copy(
            zeros, matrix_ref.at[pl.ds(index * FILL_ROWS, FILL_ROWS), :], fill_sem.at[index]
        )

    fetched = fetch(
        [
            (blocks_hbm, blocks_ref),
            (points_hbm, points_ref),
            (centres_hbm, centres_ref),
            (exponents_hbm, exponents_ref),
        ],
        fetch_sem,
    )
    zeros[...] = jnp.zeros_like(zeros)
    for index in range(fills):
        fill_copy(index).start()
    sums_ref[...] = jnp.zeros_like(sums_ref)
    fetched[0].wait()
    fetched[1].wait()
    tiles, items = list_tiles(
        sizes, blocks_ref, points_ref, tile_slot, tile_row, tile_col, item_tile, item_half
    )

    @pl.loop(0, tiles)
    def _(tile):
        tile_copy(tile).start()

    fetched[2].wait()
    fetched[3].wait()

    @pl.loop(0, tiles)
    def _(tile):
        tile_copy(tile).wait()

    def one(item):
        tile, half = item_tile[item], item_half[item]
        slot = tile_slot[tile]
        points = half_rows(points_ref[slot], half, halves)[0:3]
        rate, centre = functions_of(centres_ref, exponents_ref, tile_row[tile], tile_col[tile])
        right, left = distance_factors(points, rate, centre)
        value = jnp.exp(outer_sum(right, left))
        low = value.astype(BF16)
        panel = held[tile]
        left_sum = lax.dot_general(
            low[:, BLK:], panel, (((1,), (1,)), ((), ())), preferred_element_type=F32
        )
        right_sum = jnp.dot(low[:, :BLK], panel, preferred_element_type=F32)
        product = value * jnp.concatenate([left_sum, right_sum], axis=1)
        upper = product.astype(BF16)
        lower = (product - upper.astype(F32)).astype(BF16)
        c1, c2, c3 = parts_of(coefficients(rate, centre))
        rest = jnp.zeros((BLK - 24, 2 * BLK), F32)
        for_upper = jnp.concatenate([c1, c2, c3, rest], axis=0).astype(BF16)
        for_lower = jnp.concatenate([jnp.zeros_like(c1), c1, c2, rest], axis=0).astype(BF16)
        contract = (((1,), (1,)), ((), ()))
        terms = lax.dot_general(upper, for_upper, contract, preferred_element_type=F32)
        terms += lax.dot_general(lower, for_lower, contract, preferred_element_type=F32)
        terms = terms.T
        summed = terms[0:8] + terms[8:16] + terms[16:24]
        gradient = 2.0 * (summed[1:4] - points * summed[0:1])
        piece = jnp.concatenate([summed[4:5], gradient], axis=0)
        rows = lax.broadcasted_iota(jnp.int32, (4 * halves, BLK), 0)
        return slot, (rows >= 4 * half) & (rows < 4 * half + 4), jnp.concatenate([piece] * halves, 0)

    @pl.loop(0, lax.div(items + GROUP - 1, GROUP))
    def _(group):
        results = [one(jnp.minimum(GROUP * group + k, items - 1)) for k in range(GROUP)]
        for slot, chosen, piece in results:
            sums_ref[slot] = jnp.where(chosen, piece, sums_ref[slot])

    for index in range(fills):
        fill_copy(index).wait()


def potential_tiles(
    sizes,
    fills,
    blocks_hbm,
    centres_hbm,
    exponents_hbm,
    points_hbm,
    fields_hbm,
    extra_hbm,
    given_ref,
    matrix_ref,
    samples_ref,
    amounts_ref,
    fields_ref,
    extra_ref,
    points_ref,
    blocks_ref,
    centres_ref,
    exponents_ref,
    fetch_sem,
    total,
    zeros,
    tile_slot,
    tile_row,
    tile_col,
    item_tile,
    item_half,
    tile_goal,
    tile_sem,
    fill_sem,
):
    grid_size, col_size, batches, row_blocks, halves = sizes
    row_count, col_count = matrix_ref.shape
    first_row = lax.axis_index("grid") * row_blocks
    first_col = lax.axis_index("col") * (col_count // BLK)

    def fill_copy(index):
        return pltpu.make_async_copy(
            zeros, matrix_ref.at[pl.ds(index * FILL_ROWS, FILL_ROWS), :], fill_sem.at[index]
        )

    fetched = fetch(
        [
            (blocks_hbm, blocks_ref),
            (points_hbm, points_ref),
            (centres_hbm, centres_ref),
            (exponents_hbm, exponents_ref),
            (fields_hbm, fields_ref),
            (extra_hbm, extra_ref),
        ],
        fetch_sem,
    )
    zeros[...] = jnp.zeros_like(zeros)
    every_fill = range(fills, row_count // FILL_ROWS)
    for index in every_fill:
        fill_copy(index).start()
    fetched[0].wait()
    fetched[1].wait()
    tiles, items = list_tiles(
        sizes, blocks_ref, points_ref, tile_slot, tile_row, tile_col, item_tile, item_half
    )
    total[...] = jnp.zeros_like(total)
    for copy in fetched[2:]:
        copy.wait()

    @pl.loop(0, tiles)
    def _(tile):
        def step(k, goal):
            other = tile - 1 - k
            same = (tile_row[other] == tile_row[tile]) & (tile_col[other] == tile_col[tile])
            return jnp.where(same, other, goal)

        tile_goal[tile] = lax.fori_loop(0, tile, step, tile)

    for batch in range(batches):
        for half in range(halves):
            place = batch * halves + half
            samples_ref[batch : batch + 1, half * BLK : (half + 1) * BLK] = extra_ref[
                0, place : place + 1, :
            ]
        amounts_ref[batch] = jnp.sum(extra_ref[1, batch * halves : (batch + 1) * halves, :])

    def one(item):
        tile, half = item_tile[item], item_half[item]
        slot = tile_slot[tile]
        points = half_rows(points_ref[slot], half, halves)[0:3]
        field = half_rows(fields_ref[slot], half, halves)
        rate, centre = functions_of(centres_ref, exponents_ref, tile_row[tile], tile_col[tile])
        distance_right, distance_left = distance_factors(points, rate, centre)
        value = jnp.exp(outer_sum(distance_left, distance_right))
        slant = -2.0 * jnp.sum(field[1:4] * points, axis=0, keepdims=True)
        right = jnp.concatenate(
            [slant, 2.0 * field[1:4], field[0:1], jnp.zeros((3, BLK), F32)], axis=0
        )
        weighted = (value * outer_sum(coefficients(rate, centre), right)).astype(BF16)
        low = value.astype(BF16)
        left_side = jnp.concatenate([low[:BLK], weighted[:BLK]], axis=1)
        right_side = jnp.concatenate([weighted[BLK:], low[BLK:]], axis=1)
        return tile, lax.dot_general(
            left_side, right_side, (((1,), (1,)), ((), ())), preferred_element_type=F32
        )

    @pl.loop(0, lax.div(items + GROUP - 1, GROUP))
    def _(group):
        results = [one(jnp.minimum(GROUP * group + k, items - 1)) for k in range(GROUP)]
        for k, (tile, result) in enumerate(results):
            goal = jnp.where(GROUP * group + k < items, tile_goal[tile], grid_size)
            total[goal] += result

    for index in every_fill:
        fill_copy(index).wait()

    def tile_copy(tile):
        row = pl.multiple_of((tile_row[tile] - first_row) * BLK, BLK)
        column = pl.multiple_of((tile_col[tile] - first_col) * BLK, BLK)
        return pltpu.make_async_copy(
            total.at[tile], matrix_ref.at[pl.ds(row, BLK), pl.ds(column, BLK)], tile_sem.at[tile]
        )

    @pl.loop(0, tiles)
    def _(tile):
        @pl.when(tile_goal[tile] == tile)
        def _():
            tile_copy(tile).start()

    @pl.loop(0, tiles)
    def _(tile):
        @pl.when(tile_goal[tile] == tile)
        def _():
            tile_copy(tile).wait()


def local(density, centres, exponents, coords, weights, core_density, counts, blocks):
    grid_size = lax.axis_size("grid")
    col_size = lax.axis_size("col")
    row_count, col_count = density.shape
    batches, _, points_len = coords.shape
    row_blocks = row_count // BLK
    halves = points_len // BLK
    sizes = (grid_size, col_size, batches, row_blocks, halves)
    rates = exponents.reshape(exponents.shape[0] // BLK, BLK)
    table = blocks.T
    parts_first = coords.transpose(1, 0, 2)
    vmem = pl.BlockSpec(memory_space=pltpu.VMEM)
    smem = pl.BlockSpec(memory_space=pltpu.SMEM)
    anywhere = pl.BlockSpec(memory_space=pl.ANY)
    slot_shape = (grid_size, 4 * halves, BLK)
    hbm = pl.BlockSpec(memory_space=pltpu.HBM)
    table_memory = pltpu.SMEM(table.shape, jnp.int32)
    count_memory = pltpu.SMEM((batches,), jnp.int32)
    function_memory = [
        pltpu.VMEM(slot_shape, F32),
        table_memory,
        pltpu.VMEM(centres.shape, F32),
        pltpu.VMEM(rates.shape, F32),
        pltpu.SemaphoreType.DMA((6,)),
    ]
    slots = jax.ShapeDtypeStruct(slot_shape, F32)
    matrix = jax.ShapeDtypeStruct((row_count, col_count), F32)
    all_fills = row_count // FILL_ROWS
    fills = int(all_fills * FIRST_FILL)

    points = pl.pallas_call(
        lambda *refs: exchange_points(sizes, *refs),
        out_shape=slots,
        in_specs=[hbm, hbm, hbm],
        out_specs=anywhere,
        scratch_shapes=[
            table_memory,
            count_memory,
            pltpu.VMEM(parts_first.shape, F32),
            pltpu.VMEM((batches, 4 * halves, BLK), F32),
            pltpu.VMEM(slot_shape, F32),
            pltpu.SemaphoreType.DMA((3,)),
            pltpu.SemaphoreType.DMA,
            pltpu.SemaphoreType.DMA((grid_size,)),
            pltpu.SemaphoreType.DMA((grid_size,)),
        ],
        compiler_params=pltpu.CompilerParams(
            collective_id=0, has_side_effects=True, vmem_limit_bytes=VMEM_LIMIT
        ),
        name="exchange_points",
    )(table, counts, parts_first)

    lists = [pltpu.SMEM((grid_size + 1,), jnp.int32)] * 3 + [
        pltpu.SMEM((halves * grid_size + 1,), jnp.int32)
    ] * 2
    sums, started = pl.pallas_call(
        lambda *refs: density_tiles(sizes, fills, *refs),
        out_shape=(slots, matrix),
        in_specs=[hbm] * 5,
        out_specs=(vmem, anywhere),
        scratch_shapes=[
            *function_memory,
            pltpu.VMEM((grid_size, BLK, BLK), BF16),
            pltpu.VMEM((FILL_ROWS, col_count), F32),
            *lists,
            pltpu.SemaphoreType.DMA((grid_size,)),
            pltpu.SemaphoreType.DMA((all_fills,)),
        ],
        compiler_params=pltpu.CompilerParams(vmem_limit_bytes=VMEM_LIMIT),
        name="density_tiles",
    )(table, density, centres, rates, points)

    fields, extra = pl.pallas_call(
        lambda *refs: exchange_sums(sizes, *refs),
        out_shape=(slots, jax.ShapeDtypeStruct((2, batches * halves, BLK), F32)),
        in_specs=[hbm, hbm, hbm, hbm, hbm],
        out_specs=(anywhere, anywhere),
        scratch_shapes=[
            pltpu.VMEM(slot_shape, F32),
            table_memory,
            count_memory,
            pltpu.VMEM(weights.shape, F32),
            pltpu.VMEM(core_density.shape, F32),
            pltpu.SemaphoreType.DMA((5,)),
            pltpu.VMEM(slot_shape, F32),
            pltpu.VMEM((col_size, batches, 4 * halves, BLK), F32),
            pltpu.VMEM((batches, 4 * halves, BLK), F32),
            pltpu.VMEM(slot_shape, F32),
            pltpu.VMEM((2, batches * halves, BLK), F32),
            pltpu.SemaphoreType.DMA((2,)),
            pltpu.SemaphoreType.DMA((grid_size,)),
            pltpu.SemaphoreType.DMA((grid_size,)),
            pltpu.SemaphoreType.DMA((col_size,)),
            pltpu.SemaphoreType.DMA((col_size,)),
            pltpu.SemaphoreType.DMA((grid_size,)),
            pltpu.SemaphoreType.DMA((grid_size,)),
        ],
        compiler_params=pltpu.CompilerParams(
            collective_id=1, has_side_effects=True, vmem_limit_bytes=VMEM_LIMIT
        ),
        name="exchange_sums",
    )(table, counts, weights, core_density, sums)

    return pl.pallas_call(
        lambda *refs: potential_tiles(sizes, fills, *refs),
        out_shape=(
            matrix,
            jax.ShapeDtypeStruct((batches, points_len), F32),
            jax.ShapeDtypeStruct((batches,), F32),
        ),
        in_specs=[hbm] * 6 + [anywhere],
        out_specs=(anywhere, vmem, smem),
        scratch_shapes=[
            pltpu.VMEM(slot_shape, F32),
            pltpu.VMEM((2, batches * halves, BLK), F32),
            *function_memory,
            pltpu.VMEM((grid_size + 1, BLK, BLK), F32),
            pltpu.VMEM((FILL_ROWS, col_count), F32),
            *lists,
            pltpu.SMEM((grid_size + 1,), jnp.int32),
            pltpu.SemaphoreType.DMA((grid_size,)),
            pltpu.SemaphoreType.DMA((all_fills,)),
        ],
        input_output_aliases={6: 0},
        compiler_params=pltpu.CompilerParams(vmem_limit_bytes=VMEM_LIMIT),
        name="potential_tiles",
    )(table, centres, rates, points, fields, extra, started)


def solution(mesh):
    return jax.shard_map(
        local,
        mesh=mesh,
        in_specs=(
            P("grid", "col"),
            P(),
            P(),
            P("grid", None, None),
            P("grid", None),
            P("grid", None),
            P("grid"),
            P(),
        ),
        out_specs=(P("grid", "col"), P("grid", None), P("grid")),
        check_vma=False,
    )
```

```python
import math

import jax
import jax.numpy as jnp
from jax import lax
from jax.experimental import pallas as pl
from jax.experimental.pallas import tpu as pltpu
from jax.sharding import PartitionSpec as P

BLK = 128
FILL_ROWS = 32
FIRST_FILL = 0.5
GROUP = 4
VMEM_LIMIT = 64 * 1024 * 1024
MESH = pl.DeviceIdType.MESH
F32 = jnp.float32
BF16 = jnp.bfloat16

kappa_pbe = 0.804
mu_coef = 0.2195
slater = -0.7385587663820224
grad_scale = 4.0 * (3.0 * math.pi**2) ** (2.0 / 3.0)
soft_square = 0.25


def xc_kernel(total, grad_square):
    root = jnp.sqrt(total * total + soft_square)
    regular = 0.5 * (total + root)
    log_regular = jnp.log(regular)
    third = jnp.exp(log_regular * (1.0 / 3.0))
    four_thirds = jnp.exp(log_regular * (4.0 / 3.0))
    scaled = grad_scale * four_thirds * four_thirds
    inverse = 1.0 / (kappa_pbe * scaled + mu_coef * grad_square)
    ratio = scaled * inverse
    enhance = 1.0 + kappa_pbe - kappa_pbe * kappa_pbe * ratio
    energy = slater * four_thirds * enhance
    inner = (4.0 / 3.0) * enhance - (8.0 / 3.0) * kappa_pbe * kappa_pbe * ratio * (
        mu_coef * grad_square * inverse
    )
    deriv_density = slater * third * inner * (0.5 * (1.0 + total / root))
    deriv_sigma = slater * four_thirds * (kappa_pbe * kappa_pbe * mu_coef) * ratio * inverse
    return energy, deriv_density, deriv_sigma


def parts_of(value):
    first = value.astype(BF16).astype(F32)
    rest = value - first
    second = rest.astype(BF16).astype(F32)
    return first, second, rest - second


def outer_sum(left, right):
    l1, l2, l3 = parts_of(left)
    r1, r2, r3 = parts_of(right)
    lefts = jnp.concatenate([l1, l1, l1, l2, l2, l3], axis=0).astype(BF16)
    rights = jnp.concatenate([r1, r2, r3, r1, r2, r1], axis=0).astype(BF16)
    return lax.dot_general(
        lefts, rights, (((0,), (0,)), ((), ())), preferred_element_type=F32
    )


def batch_of(blocks_ref, requester, entry, owner, batches, row_blocks):
    found = jnp.int32(-1)
    for batch in range(batches):
        offset = blocks_ref[entry, requester * batches + batch] - owner * row_blocks
        found = jnp.where((offset >= 0) & (offset < row_blocks), batch, found)
    return found


def owners_of(sizes, blocks_ref, requester):
    grid_size, col_size, batches, row_blocks, halves = sizes
    return [
        [lax.div(blocks_ref[entry, requester * batches + batch], row_blocks) for batch in range(batches)]
        for entry in range(col_size)
    ]


def asked_batch(sizes, owners, owner):
    grid_size, col_size, batches, row_blocks, halves = sizes
    found = jnp.int32(0)
    for batch in range(1, batches):
        found = jnp.where(owners[owner // (grid_size // col_size)][batch] == owner, batch, found)
    return found


def fetch(pairs, sems):
    copies = [
        pltpu.make_async_copy(source, target, sems.at[place])
        for place, (source, target) in enumerate(pairs)
    ]
    for copy in copies:
        copy.start()
    return copies


def exchange_points(
    sizes,
    blocks_hbm,
    counts_hbm,
    coords_hbm,
    out_ref,
    blocks_ref,
    counts_ref,
    coords_ref,
    packed,
    staged,
    fetch_sem,
    own_sem,
    send,
    recv,
):
    grid_size, col_size, batches, row_blocks, halves = sizes
    me, col = lax.axis_index("grid"), lax.axis_index("col")
    fetched = fetch(
        [(blocks_hbm, blocks_ref), (counts_hbm, counts_ref), (coords_hbm, coords_ref)], fetch_sem
    )
    barrier = pltpu.get_barrier_semaphore()
    for step in range(1, grid_size):
        other = lax.rem(me + step, grid_size)
        pl.semaphore_signal(barrier, inc=1, device_id=(other, col), device_id_type=MESH)
    for copy in fetched:
        copy.wait()
    points = coords_ref[...]
    for batch in range(batches):
        count = jnp.full((1, BLK), counts_ref[batch].astype(F32), F32)
        pieces = []
        for half in range(halves):
            lanes = slice(half * BLK, (half + 1) * BLK)
            pieces += [points[d, batch : batch + 1, lanes] for d in range(3)] + [count]
        packed[batch] = jnp.concatenate(pieces, axis=0)
    owners = owners_of(sizes, blocks_ref, me)
    for owner in range(grid_size):
        staged[owner] = packed[asked_batch(sizes, owners, owner)]
    pl.semaphore_wait(barrier, grid_size - 1)
    copies = []
    for step in range(1, grid_size):
        other = lax.rem(me + step, grid_size)
        copy = pltpu.make_async_remote_copy(
            src_ref=staged.at[other],
            dst_ref=out_ref.at[me],
            send_sem=send.at[step],
            recv_sem=recv.at[step],
            device_id=(other, col),
            device_id_type=MESH,
        )
        copy.start()
        copies.append(copy)
    own = pltpu.make_async_copy(staged.at[me], out_ref.at[me], own_sem)
    own.start()
    for copy in copies:
        copy.wait_recv()
    for copy in copies:
        copy.wait_send()
    own.wait()


def exchange_sums(
    sizes,
    blocks_hbm,
    counts_hbm,
    weights_hbm,
    core_hbm,
    sums_hbm,
    out_ref,
    extra_ref,
    sums_ref,
    blocks_ref,
    counts_ref,
    weights_ref,
    core_ref,
    fetch_sem,
    landed,
    col_sums,
    fields,
    staged,
    extra,
    own_sem,
    send_a,
    recv_a,
    send_b,
    recv_b,
    send_c,
    recv_c,
):
    grid_size, col_size, batches, row_blocks, halves = sizes
    me, col = lax.axis_index("grid"), lax.axis_index("col")
    fetched = fetch(
        [
            (blocks_hbm, blocks_ref),
            (counts_hbm, counts_ref),
            (weights_hbm, weights_ref),
            (core_hbm, core_ref),
            (sums_hbm, sums_ref),
        ],
        fetch_sem,
    )
    barrier = pltpu.get_barrier_semaphore()
    for step in range(1, grid_size):
        other = lax.rem(me + step, grid_size)
        pl.semaphore_signal(barrier, inc=1, device_id=(other, col), device_id_type=MESH)
    for step in range(1, col_size):
        other = lax.rem(col + step, col_size)
        pl.semaphore_signal(barrier, inc=1, device_id=(me, other), device_id_type=MESH)
    for copy in fetched:
        copy.wait()
    owners = owners_of(sizes, blocks_ref, me)
    asked = [asked_batch(sizes, owners, owner) for owner in range(grid_size)]
    pl.semaphore_wait(barrier, grid_size + col_size - 2)

    copies = []
    for step in range(1, grid_size):
        other = lax.rem(me + step, grid_size)
        copy = pltpu.make_async_remote_copy(
            src_ref=sums_ref.at[other],
            dst_ref=landed.at[me],
            send_sem=send_a.at[step],
            recv_sem=recv_a.at[step],
            device_id=(other, col),
            device_id_type=MESH,
        )
        copy.start()
        copies.append(copy)
    kept = fetch([(sums_ref.at[me], landed.at[me])], own_sem)
    for copy in copies:
        copy.wait_recv()
    kept[0].wait()
    sent = copies

    for batch in range(batches):
        total = None
        for entry in range(col_size):
            term = landed[owners[entry][batch]]
            total = term if total is None else total + term
        col_sums[col, batch] = total
    copies = []
    for step in range(1, col_size):
        other = lax.rem(col + step, col_size)
        copy = pltpu.make_async_remote_copy(
            src_ref=col_sums.at[col],
            dst_ref=col_sums.at[col],
            send_sem=send_b.at[step],
            recv_sem=recv_b.at[step],
            device_id=(me, other),
            device_id_type=MESH,
        )
        copy.start()
        copies.append(copy)
    for copy in copies:
        copy.wait_recv()
    sent += copies
    summed = col_sums[0]
    for entry in range(1, col_size):
        summed = summed + col_sums[entry]

    places = [(batch, half) for batch in range(batches) for half in range(halves)]

    def rows_of(field):
        return jnp.concatenate(
            [summed[batch, 4 * half + field : 4 * half + field + 1] for batch, half in places],
            axis=0,
        )

    def rows_in(ref):
        value = ref[...]
        return jnp.concatenate(
            [value[batch : batch + 1, half * BLK : (half + 1) * BLK] for batch, half in places],
            axis=0,
        )

    lanes = lax.broadcasted_iota(jnp.int32, (1, BLK), 1)
    live = jnp.concatenate(
        [jnp.where(lanes + half * BLK < counts_ref[batch], 1.0, 0.0) for batch, half in places],
        axis=0,
    )
    valence = jnp.where(live > 0.0, rows_of(0), 0.0)
    gradient = [jnp.where(live > 0.0, rows_of(1 + d), 0.0) for d in range(3)]
    grad_square = (
        gradient[0] * gradient[0] + gradient[1] * gradient[1] + gradient[2] * gradient[2]
    )
    energy, deriv_density, deriv_sigma = xc_kernel(valence + rows_in(core_ref), grad_square)
    point_scale = rows_in(weights_ref) * live
    spread = 2.0 * point_scale * deriv_sigma
    table = [point_scale * deriv_density] + [spread * gradient[d] for d in range(3)]
    for batch in range(batches):
        fields[batch] = jnp.concatenate(
            [
                table[k][batch * halves + half : batch * halves + half + 1]
                for half in range(halves)
                for k in range(4)
            ],
            axis=0,
        )
    for owner in range(grid_size):
        staged[owner] = fields[asked[owner]]
    copies = []
    for step in range(1, grid_size):
        other = lax.rem(me + step, grid_size)
        copy = pltpu.make_async_remote_copy(
            src_ref=staged.at[other],
            dst_ref=out_ref.at[me],
            send_sem=send_c.at[step],
            recv_sem=recv_c.at[step],
            device_id=(other, col),
            device_id_type=MESH,
        )
        copy.start()
        copies.append(copy)
    extra[0] = valence
    extra[1] = point_scale * energy
    kept = fetch([(staged.at[me], out_ref.at[me]), (extra, extra_ref)], own_sem)
    for copy in copies:
        copy.wait_recv()
    for copy in sent + copies:
        copy.wait_send()
    for copy in kept:
        copy.wait()


def list_tiles(sizes, blocks_ref, points_ref, tile_slot, tile_row, tile_col, item_tile, item_half):
    grid_size, col_size, batches, row_blocks, halves = sizes
    me, col = lax.axis_index("grid"), lax.axis_index("col")
    entry = lax.div(me, grid_size // col_size)

    def step(slot, carry):
        tiles, items = carry
        found = batch_of(blocks_ref, slot, entry, me, batches, row_blocks)
        batch = jnp.maximum(found, 0)
        has = found >= 0
        tile_slot[tiles] = slot
        tile_row[tiles] = blocks_ref[entry, slot * batches + batch]
        tile_col[tiles] = blocks_ref[col, slot * batches + batch]
        count = points_ref[slot, 3, 0]
        for half in range(halves):
            item_tile[items] = tiles
            item_half[items] = half
            items = items + jnp.where(has & (count > half * BLK), 1, 0)
        return tiles + jnp.where(has, 1, 0), items

    return lax.fori_loop(0, grid_size, step, (jnp.int32(0), jnp.int32(0)), unroll=True)


def half_rows(value, half, halves):
    picked = value[0:4]
    for other in range(1, halves):
        picked = jnp.where(half == other, value[4 * other : 4 * other + 4], picked)
    return picked


def functions_of(centres_ref, exponents_ref, row, column):
    rate = jnp.concatenate(
        [exponents_ref[pl.ds(row, 1), :], exponents_ref[pl.ds(column, 1), :]], axis=1
    )
    centre = jnp.concatenate(
        [
            centres_ref[:, pl.ds(pl.multiple_of(row * BLK, BLK), BLK)],
            centres_ref[:, pl.ds(pl.multiple_of(column * BLK, BLK), BLK)],
        ],
        axis=1,
    )
    return rate, centre


def distance_factors(points, rate, centre):
    square = jnp.sum(points * points, axis=0, keepdims=True)
    right = jnp.concatenate(
        [square, points, jnp.ones((1, BLK), F32), jnp.zeros((3, BLK), F32)], axis=0
    )
    left = jnp.concatenate(
        [
            -rate,
            2.0 * rate * centre,
            -rate * jnp.sum(centre * centre, axis=0, keepdims=True),
            jnp.zeros((3, 2 * BLK), F32),
        ],
        axis=0,
    )
    return right, left


def coefficients(rate, centre):
    lanes = lax.broadcasted_iota(jnp.int32, (1, 2 * BLK), 1)
    return jnp.concatenate(
        [
            rate,
            rate * centre,
            jnp.where(lanes >= BLK, 1.0, 0.0),
            jnp.zeros((3, 2 * BLK), F32),
        ],
        axis=0,
    )


def density_tiles(
    sizes,
    fills,
    blocks_hbm,
    density_ref,
    centres_hbm,
    exponents_hbm,
    points_hbm,
    sums_hbm,
    matrix_ref,
    sums_ref,
    out_sem,
    points_ref,
    blocks_ref,
    centres_ref,
    exponents_ref,
    fetch_sem,
    held,
    zeros,
    tile_slot,
    tile_row,
    tile_col,
    item_tile,
    item_half,
    tile_sem,
    fill_sem,
):
    grid_size, col_size, batches, row_blocks, halves = sizes
    col_blocks = density_ref.shape[1] // BLK
    first_row = lax.axis_index("grid") * row_blocks
    first_col = lax.axis_index("col") * col_blocks

    def tile_copy(tile):
        row = pl.multiple_of((tile_row[tile] - first_row) * BLK, BLK)
        column = pl.multiple_of((tile_col[tile] - first_col) * BLK, BLK)
        return pltpu.make_async_copy(
            density_ref.at[pl.ds(row, BLK), pl.ds(column, BLK)], held.at[tile], tile_sem.at[tile]
        )

    def fill_copy(index):
        return pltpu.make_async_copy(
            zeros, matrix_ref.at[pl.ds(index * FILL_ROWS, FILL_ROWS), :], fill_sem.at[index]
        )

    fetched = fetch(
        [
            (blocks_hbm, blocks_ref),
            (points_hbm, points_ref),
            (centres_hbm, centres_ref),
            (exponents_hbm, exponents_ref),
        ],
        fetch_sem,
    )
    zeros[...] = jnp.zeros_like(zeros)
    for index in range(fills):
        fill_copy(index).start()
    sums_ref[...] = jnp.zeros_like(sums_ref)
    fetched[0].wait()
    fetched[1].wait()
    tiles, items = list_tiles(
        sizes, blocks_ref, points_ref, tile_slot, tile_row, tile_col, item_tile, item_half
    )

    @pl.loop(0, tiles)
    def _(tile):
        tile_copy(tile).start()

    fetched[2].wait()
    fetched[3].wait()

    @pl.loop(0, tiles)
    def _(tile):
        tile_copy(tile).wait()

    def one(item):
        tile, half = item_tile[item], item_half[item]
        slot = tile_slot[tile]
        points = half_rows(points_ref[slot], half, halves)[0:3]
        rate, centre = functions_of(centres_ref, exponents_ref, tile_row[tile], tile_col[tile])
        right, left = distance_factors(points, rate, centre)
        value = jnp.exp(outer_sum(right, left))
        low = value.astype(BF16)
        panel = held[tile]
        left_sum = lax.dot_general(
            low[:, BLK:], panel, (((1,), (1,)), ((), ())), preferred_element_type=F32
        )
        right_sum = jnp.dot(low[:, :BLK], panel, preferred_element_type=F32)
        product = value * jnp.concatenate([left_sum, right_sum], axis=1)
        upper = product.astype(BF16)
        lower = (product - upper.astype(F32)).astype(BF16)
        c1, c2, c3 = parts_of(coefficients(rate, centre))
        rest = jnp.zeros((BLK - 24, 2 * BLK), F32)
        for_upper = jnp.concatenate([c1, c2, c3, rest], axis=0).astype(BF16)
        for_lower = jnp.concatenate([jnp.zeros_like(c1), c1, c2, rest], axis=0).astype(BF16)
        contract = (((1,), (1,)), ((), ()))
        terms = lax.dot_general(upper, for_upper, contract, preferred_element_type=F32)
        terms += lax.dot_general(lower, for_lower, contract, preferred_element_type=F32)
        terms = terms.T
        summed = terms[0:8] + terms[8:16] + terms[16:24]
        gradient = 2.0 * (summed[1:4] - points * summed[0:1])
        piece = jnp.concatenate([summed[4:5], gradient], axis=0)
        rows = lax.broadcasted_iota(jnp.int32, (4 * halves, BLK), 0)
        return slot, (rows >= 4 * half) & (rows < 4 * half + 4), jnp.concatenate([piece] * halves, 0)

    @pl.loop(0, lax.div(items + GROUP - 1, GROUP))
    def _(group):
        results = [one(jnp.minimum(GROUP * group + k, items - 1)) for k in range(GROUP)]
        for slot, chosen, piece in results:
            sums_ref[slot] = jnp.where(chosen, piece, sums_ref[slot])

    out = pltpu.make_async_copy(sums_ref, sums_hbm, out_sem)
    out.start()
    for index in range(fills):
        fill_copy(index).wait()
    out.wait()


def potential_tiles(
    sizes,
    fills,
    blocks_hbm,
    centres_hbm,
    exponents_hbm,
    points_hbm,
    fields_hbm,
    extra_hbm,
    given_ref,
    matrix_ref,
    samples_hbm,
    amounts_hbm,
    samples_ref,
    amounts_ref,
    out_sem,
    fields_ref,
    extra_ref,
    points_ref,
    blocks_ref,
    centres_ref,
    exponents_ref,
    fetch_sem,
    total,
    zeros,
    tile_slot,
    tile_row,
    tile_col,
    item_tile,
    item_half,
    tile_goal,
    tile_sem,
    fill_sem,
):
    grid_size, col_size, batches, row_blocks, halves = sizes
    row_count, col_count = matrix_ref.shape
    first_row = lax.axis_index("grid") * row_blocks
    first_col = lax.axis_index("col") * (col_count // BLK)

    def fill_copy(index):
        return pltpu.make_async_copy(
            zeros, matrix_ref.at[pl.ds(index * FILL_ROWS, FILL_ROWS), :], fill_sem.at[index]
        )

    fetched = fetch(
        [
            (blocks_hbm, blocks_ref),
            (points_hbm, points_ref),
            (centres_hbm, centres_ref),
            (exponents_hbm, exponents_ref),
            (fields_hbm, fields_ref),
            (extra_hbm, extra_ref),
        ],
        fetch_sem,
    )
    zeros[...] = jnp.zeros_like(zeros)
    every_fill = range(fills, row_count // FILL_ROWS)
    for index in every_fill:
        fill_copy(index).start()
    fetched[0].wait()
    fetched[1].wait()
    tiles, items = list_tiles(
        sizes, blocks_ref, points_ref, tile_slot, tile_row, tile_col, item_tile, item_half
    )
    total[...] = jnp.zeros_like(total)
    for copy in fetched[2:]:
        copy.wait()

    @pl.loop(0, tiles)
    def _(tile):
        def step(k, goal):
            other = tile - 1 - k
            same = (tile_row[other] == tile_row[tile]) & (tile_col[other] == tile_col[tile])
            return jnp.where(same, other, goal)

        tile_goal[tile] = lax.fori_loop(0, tile, step, tile)

    for batch in range(batches):
        for half in range(halves):
            place = batch * halves + half
            samples_ref[batch : batch + 1, half * BLK : (half + 1) * BLK] = extra_ref[
                0, place : place + 1, :
            ]
        amounts_ref[batch] = jnp.sum(extra_ref[1, batch * halves : (batch + 1) * halves, :])
    outs = fetch([(samples_ref, samples_hbm), (amounts_ref, amounts_hbm)], out_sem)

    def one(item):
        tile, half = item_tile[item], item_half[item]
        slot = tile_slot[tile]
        points = half_rows(points_ref[slot], half, halves)[0:3]
        field = half_rows(fields_ref[slot], half, halves)
        rate, centre = functions_of(centres_ref, exponents_ref, tile_row[tile], tile_col[tile])
        distance_right, distance_left = distance_factors(points, rate, centre)
        value = jnp.exp(outer_sum(distance_left, distance_right))
        slant = -2.0 * jnp.sum(field[1:4] * points, axis=0, keepdims=True)
        right = jnp.concatenate(
            [slant, 2.0 * field[1:4], field[0:1], jnp.zeros((3, BLK), F32)], axis=0
        )
        weighted = (value * outer_sum(coefficients(rate, centre), right)).astype(BF16)
        low = value.astype(BF16)
        left_side = jnp.concatenate([low[:BLK], weighted[:BLK]], axis=1)
        right_side = jnp.concatenate([weighted[BLK:], low[BLK:]], axis=1)
        return tile, lax.dot_general(
            left_side, right_side, (((1,), (1,)), ((), ())), preferred_element_type=F32
        )

    @pl.loop(0, lax.div(items + GROUP - 1, GROUP))
    def _(group):
        results = [one(jnp.minimum(GROUP * group + k, items - 1)) for k in range(GROUP)]
        for k, (tile, result) in enumerate(results):
            goal = jnp.where(GROUP * group + k < items, tile_goal[tile], grid_size)
            total[goal] += result


    def tile_copy(tile):
        row = pl.multiple_of((tile_row[tile] - first_row) * BLK, BLK)
        column = pl.multiple_of((tile_col[tile] - first_col) * BLK, BLK)
        return pltpu.make_async_copy(
            total.at[tile], matrix_ref.at[pl.ds(row, BLK), pl.ds(column, BLK)], tile_sem.at[tile]
        )

    def write_rows(first, last):
        @pl.loop(0, tiles)
        def _(tile):
            row = tile_row[tile] - first_row

            @pl.when((tile_goal[tile] == tile) & (row >= first) & (row < last))
            def _():
                tile_copy(tile).start()

    per_block = BLK // FILL_ROWS
    ready = fills // per_block
    write_rows(0, ready)
    for block in range(ready, row_blocks):
        for index in range(max(block * per_block, fills), (block + 1) * per_block):
            fill_copy(index).wait()
        if block % 2 == 1 or block == row_blocks - 1:
            write_rows(max(ready, block - block % 2), block + 1)

    @pl.loop(0, tiles)
    def _(tile):
        @pl.when(tile_goal[tile] == tile)
        def _():
            tile_copy(tile).wait()

    for copy in outs:
        copy.wait()


def local(density, centres, exponents, coords, weights, core_density, counts, blocks):
    grid_size = lax.axis_size("grid")
    col_size = lax.axis_size("col")
    row_count, col_count = density.shape
    batches, _, points_len = coords.shape
    row_blocks = row_count // BLK
    halves = points_len // BLK
    sizes = (grid_size, col_size, batches, row_blocks, halves)
    rates = exponents.reshape(exponents.shape[0] // BLK, BLK)
    table = blocks.T
    parts_first = coords.transpose(1, 0, 2)
    vmem = pl.BlockSpec(memory_space=pltpu.VMEM)
    smem = pl.BlockSpec(memory_space=pltpu.SMEM)
    anywhere = pl.BlockSpec(memory_space=pl.ANY)
    slot_shape = (grid_size, 4 * halves, BLK)
    hbm = pl.BlockSpec(memory_space=pltpu.HBM)
    table_memory = pltpu.SMEM(table.shape, jnp.int32)
    count_memory = pltpu.SMEM((batches,), jnp.int32)
    function_memory = [
        pltpu.VMEM(slot_shape, F32),
        table_memory,
        pltpu.VMEM(centres.shape, F32),
        pltpu.VMEM(rates.shape, F32),
        pltpu.SemaphoreType.DMA((6,)),
    ]
    slots = jax.ShapeDtypeStruct(slot_shape, F32)
    matrix = jax.ShapeDtypeStruct((row_count, col_count), F32)
    all_fills = row_count // FILL_ROWS
    fills = int(all_fills * FIRST_FILL)

    points = pl.pallas_call(
        lambda *refs: exchange_points(sizes, *refs),
        out_shape=slots,
        in_specs=[hbm, hbm, hbm],
        out_specs=anywhere,
        scratch_shapes=[
            table_memory,
            count_memory,
            pltpu.VMEM(parts_first.shape, F32),
            pltpu.VMEM((batches, 4 * halves, BLK), F32),
            pltpu.VMEM(slot_shape, F32),
            pltpu.SemaphoreType.DMA((3,)),
            pltpu.SemaphoreType.DMA,
            pltpu.SemaphoreType.DMA((grid_size,)),
            pltpu.SemaphoreType.DMA((grid_size,)),
        ],
        compiler_params=pltpu.CompilerParams(
            collective_id=0, has_side_effects=True, vmem_limit_bytes=VMEM_LIMIT
        ),
        name="exchange_points",
    )(table, counts, parts_first)

    lists = [pltpu.SMEM((grid_size + 1,), jnp.int32)] * 3 + [
        pltpu.SMEM((halves * grid_size + 1,), jnp.int32)
    ] * 2
    sums, started = pl.pallas_call(
        lambda *refs: density_tiles(sizes, fills, *refs),
        out_shape=(slots, matrix),
        in_specs=[hbm] * 5,
        out_specs=(anywhere, anywhere),
        scratch_shapes=[
            pltpu.VMEM(slot_shape, F32),
            pltpu.SemaphoreType.DMA,
            *function_memory,
            pltpu.VMEM((grid_size, BLK, BLK), BF16),
            pltpu.VMEM((FILL_ROWS, col_count), F32),
            *lists,
            pltpu.SemaphoreType.DMA((grid_size,)),
            pltpu.SemaphoreType.DMA((all_fills,)),
        ],
        compiler_params=pltpu.CompilerParams(vmem_limit_bytes=VMEM_LIMIT),
        name="density_tiles",
    )(table, density, centres, rates, points)

    fields, extra = pl.pallas_call(
        lambda *refs: exchange_sums(sizes, *refs),
        out_shape=(slots, jax.ShapeDtypeStruct((2, batches * halves, BLK), F32)),
        in_specs=[hbm, hbm, hbm, hbm, hbm],
        out_specs=(anywhere, anywhere),
        scratch_shapes=[
            pltpu.VMEM(slot_shape, F32),
            table_memory,
            count_memory,
            pltpu.VMEM(weights.shape, F32),
            pltpu.VMEM(core_density.shape, F32),
            pltpu.SemaphoreType.DMA((5,)),
            pltpu.VMEM(slot_shape, F32),
            pltpu.VMEM((col_size, batches, 4 * halves, BLK), F32),
            pltpu.VMEM((batches, 4 * halves, BLK), F32),
            pltpu.VMEM(slot_shape, F32),
            pltpu.VMEM((2, batches * halves, BLK), F32),
            pltpu.SemaphoreType.DMA((2,)),
            pltpu.SemaphoreType.DMA((grid_size,)),
            pltpu.SemaphoreType.DMA((grid_size,)),
            pltpu.SemaphoreType.DMA((col_size,)),
            pltpu.SemaphoreType.DMA((col_size,)),
            pltpu.SemaphoreType.DMA((grid_size,)),
            pltpu.SemaphoreType.DMA((grid_size,)),
        ],
        compiler_params=pltpu.CompilerParams(
            collective_id=1, has_side_effects=True, vmem_limit_bytes=VMEM_LIMIT
        ),
        name="exchange_sums",
    )(table, counts, weights, core_density, sums)

    return pl.pallas_call(
        lambda *refs: potential_tiles(sizes, fills, *refs),
        out_shape=(
            matrix,
            jax.ShapeDtypeStruct((batches, points_len), F32),
            jax.ShapeDtypeStruct((batches,), F32),
        ),
        in_specs=[hbm] * 6 + [anywhere],
        out_specs=(anywhere, anywhere, anywhere),
        scratch_shapes=[
            pltpu.VMEM((batches, points_len), F32),
            pltpu.SMEM((batches,), F32),
            pltpu.SemaphoreType.DMA((2,)),
            pltpu.VMEM(slot_shape, F32),
            pltpu.VMEM((2, batches * halves, BLK), F32),
            *function_memory,
            pltpu.VMEM((grid_size + 1, BLK, BLK), F32),
            pltpu.VMEM((FILL_ROWS, col_count), F32),
            *lists,
            pltpu.SMEM((grid_size + 1,), jnp.int32),
            pltpu.SemaphoreType.DMA((grid_size,)),
            pltpu.SemaphoreType.DMA((all_fills,)),
        ],
        input_output_aliases={6: 0},
        compiler_params=pltpu.CompilerParams(vmem_limit_bytes=VMEM_LIMIT),
        name="potential_tiles",
    )(table, centres, rates, points, fields, extra, started)


def solution(mesh):
    return jax.shard_map(
        local,
        mesh=mesh,
        in_specs=(
            P("grid", "col"),
            P(),
            P(),
            P("grid", None, None),
            P("grid", None),
            P("grid", None),
            P("grid"),
            P(),
        ),
        out_specs=(P("grid", "col"), P("grid", None), P("grid")),
        check_vma=False,
    )
```

```python
import math

import jax
import jax.numpy as jnp
from jax import lax
from jax.experimental import pallas as pl
from jax.experimental.pallas import tpu as pltpu
from jax.sharding import PartitionSpec as P

BLK = 128
FILL_ROWS = 32
FIRST_FILL = 0.6
GROUP = 4
VMEM_LIMIT = 64 * 1024 * 1024
MESH = pl.DeviceIdType.MESH
F32 = jnp.float32
BF16 = jnp.bfloat16

kappa_pbe = 0.804
mu_coef = 0.2195
slater = -0.7385587663820224
grad_scale = 4.0 * (3.0 * math.pi**2) ** (2.0 / 3.0)
soft_square = 0.25


def xc_kernel(total, grad_square):
    root = jnp.sqrt(total * total + soft_square)
    regular = 0.5 * (total + root)
    log_regular = jnp.log(regular)
    third = jnp.exp(log_regular * (1.0 / 3.0))
    four_thirds = jnp.exp(log_regular * (4.0 / 3.0))
    scaled = grad_scale * four_thirds * four_thirds
    inverse = 1.0 / (kappa_pbe * scaled + mu_coef * grad_square)
    ratio = scaled * inverse
    enhance = 1.0 + kappa_pbe - kappa_pbe * kappa_pbe * ratio
    energy = slater * four_thirds * enhance
    inner = (4.0 / 3.0) * enhance - (8.0 / 3.0) * kappa_pbe * kappa_pbe * ratio * (
        mu_coef * grad_square * inverse
    )
    deriv_density = slater * third * inner * (0.5 * (1.0 + total / root))
    deriv_sigma = slater * four_thirds * (kappa_pbe * kappa_pbe * mu_coef) * ratio * inverse
    return energy, deriv_density, deriv_sigma


def parts_of(value):
    first = value.astype(BF16).astype(F32)
    rest = value - first
    second = rest.astype(BF16).astype(F32)
    return first, second, rest - second


def outer_sum(left, right):
    l1, l2, l3 = parts_of(left)
    r1, r2, r3 = parts_of(right)
    lefts = jnp.concatenate([l1, l1, l1, l2, l2, l3], axis=0).astype(BF16)
    rights = jnp.concatenate([r1, r2, r3, r1, r2, r1], axis=0).astype(BF16)
    return lax.dot_general(
        lefts, rights, (((0,), (0,)), ((), ())), preferred_element_type=F32
    )


def batch_of(blocks_ref, requester, entry, owner, batches, row_blocks):
    found = jnp.int32(-1)
    for batch in range(batches):
        offset = blocks_ref[entry, requester * batches + batch] - owner * row_blocks
        found = jnp.where((offset >= 0) & (offset < row_blocks), batch, found)
    return found


def owners_of(sizes, blocks_ref, requester):
    grid_size, col_size, batches, row_blocks, halves = sizes
    return [
        [lax.div(blocks_ref[entry, requester * batches + batch], row_blocks) for batch in range(batches)]
        for entry in range(col_size)
    ]


def asked_batch(sizes, owners, owner):
    grid_size, col_size, batches, row_blocks, halves = sizes
    found = jnp.int32(0)
    for batch in range(1, batches):
        found = jnp.where(owners[owner // (grid_size // col_size)][batch] == owner, batch, found)
    return found


def fetch(pairs, sems):
    copies = [
        pltpu.make_async_copy(source, target, sems.at[place])
        for place, (source, target) in enumerate(pairs)
    ]
    for copy in copies:
        copy.start()
    return copies


def exchange_points(
    sizes,
    blocks_hbm,
    counts_hbm,
    coords_hbm,
    out_ref,
    blocks_ref,
    counts_ref,
    coords_ref,
    packed,
    staged,
    fetch_sem,
    own_sem,
    send,
    recv,
):
    grid_size, col_size, batches, row_blocks, halves = sizes
    me, col = lax.axis_index("grid"), lax.axis_index("col")
    fetched = fetch(
        [(blocks_hbm, blocks_ref), (counts_hbm, counts_ref), (coords_hbm, coords_ref)], fetch_sem
    )
    barrier = pltpu.get_barrier_semaphore()
    for step in range(1, grid_size):
        other = lax.rem(me + step, grid_size)
        pl.semaphore_signal(barrier, inc=1, device_id=(other, col), device_id_type=MESH)
    for copy in fetched:
        copy.wait()
    points = coords_ref[...]
    for batch in range(batches):
        count = jnp.full((1, BLK), counts_ref[batch].astype(F32), F32)
        pieces = []
        for half in range(halves):
            lanes = slice(half * BLK, (half + 1) * BLK)
            pieces += [points[d, batch : batch + 1, lanes] for d in range(3)] + [count]
        packed[batch] = jnp.concatenate(pieces, axis=0)
    owners = owners_of(sizes, blocks_ref, me)
    for owner in range(grid_size):
        staged[owner] = packed[asked_batch(sizes, owners, owner)]
    pl.semaphore_wait(barrier, grid_size - 1)
    copies = []
    for step in range(1, grid_size):
        other = lax.rem(me + step, grid_size)
        copy = pltpu.make_async_remote_copy(
            src_ref=staged.at[other],
            dst_ref=out_ref.at[me],
            send_sem=send.at[step],
            recv_sem=recv.at[step],
            device_id=(other, col),
            device_id_type=MESH,
        )
        copy.start()
        copies.append(copy)
    own = pltpu.make_async_copy(staged.at[me], out_ref.at[me], own_sem)
    own.start()
    for copy in copies:
        copy.wait_recv()
    for copy in copies:
        copy.wait_send()
    own.wait()


def exchange_sums(
    sizes,
    blocks_hbm,
    counts_hbm,
    weights_hbm,
    core_hbm,
    sums_hbm,
    out_ref,
    extra_ref,
    sums_ref,
    blocks_ref,
    counts_ref,
    weights_ref,
    core_ref,
    fetch_sem,
    landed,
    col_sums,
    fields,
    staged,
    extra,
    own_sem,
    send_a,
    recv_a,
    send_b,
    recv_b,
    send_c,
    recv_c,
):
    grid_size, col_size, batches, row_blocks, halves = sizes
    me, col = lax.axis_index("grid"), lax.axis_index("col")
    fetched = fetch(
        [
            (blocks_hbm, blocks_ref),
            (counts_hbm, counts_ref),
            (weights_hbm, weights_ref),
            (core_hbm, core_ref),
            (sums_hbm, sums_ref),
        ],
        fetch_sem,
    )
    barrier = pltpu.get_barrier_semaphore()
    for step in range(1, grid_size):
        other = lax.rem(me + step, grid_size)
        pl.semaphore_signal(barrier, inc=1, device_id=(other, col), device_id_type=MESH)
    for step in range(1, col_size):
        other = lax.rem(col + step, col_size)
        pl.semaphore_signal(barrier, inc=1, device_id=(me, other), device_id_type=MESH)
    for copy in fetched:
        copy.wait()
    owners = owners_of(sizes, blocks_ref, me)
    asked = [asked_batch(sizes, owners, owner) for owner in range(grid_size)]
    pl.semaphore_wait(barrier, grid_size + col_size - 2)

    copies = []
    for step in range(1, grid_size):
        other = lax.rem(me + step, grid_size)
        copy = pltpu.make_async_remote_copy(
            src_ref=sums_ref.at[other],
            dst_ref=landed.at[me],
            send_sem=send_a.at[step],
            recv_sem=recv_a.at[step],
            device_id=(other, col),
            device_id_type=MESH,
        )
        copy.start()
        copies.append(copy)
    kept = fetch([(sums_ref.at[me], landed.at[me])], own_sem)
    for copy in copies:
        copy.wait_recv()
    kept[0].wait()
    sent = copies

    for batch in range(batches):
        total = None
        for entry in range(col_size):
            term = landed[owners[entry][batch]]
            total = term if total is None else total + term
        col_sums[col, batch] = total
    copies = []
    for step in range(1, col_size):
        other = lax.rem(col + step, col_size)
        copy = pltpu.make_async_remote_copy(
            src_ref=col_sums.at[col],
            dst_ref=col_sums.at[col],
            send_sem=send_b.at[step],
            recv_sem=recv_b.at[step],
            device_id=(me, other),
            device_id_type=MESH,
        )
        copy.start()
        copies.append(copy)
    for copy in copies:
        copy.wait_recv()
    sent += copies
    summed = col_sums[0]
    for entry in range(1, col_size):
        summed = summed + col_sums[entry]

    places = [(batch, half) for batch in range(batches) for half in range(halves)]

    def rows_of(field):
        return jnp.concatenate(
            [summed[batch, 4 * half + field : 4 * half + field + 1] for batch, half in places],
            axis=0,
        )

    def rows_in(ref):
        value = ref[...]
        return jnp.concatenate(
            [value[batch : batch + 1, half * BLK : (half + 1) * BLK] for batch, half in places],
            axis=0,
        )

    lanes = lax.broadcasted_iota(jnp.int32, (1, BLK), 1)
    live = jnp.concatenate(
        [jnp.where(lanes + half * BLK < counts_ref[batch], 1.0, 0.0) for batch, half in places],
        axis=0,
    )
    valence = jnp.where(live > 0.0, rows_of(0), 0.0)
    gradient = [jnp.where(live > 0.0, rows_of(1 + d), 0.0) for d in range(3)]
    grad_square = (
        gradient[0] * gradient[0] + gradient[1] * gradient[1] + gradient[2] * gradient[2]
    )
    energy, deriv_density, deriv_sigma = xc_kernel(valence + rows_in(core_ref), grad_square)
    point_scale = rows_in(weights_ref) * live
    spread = 2.0 * point_scale * deriv_sigma
    table = [point_scale * deriv_density] + [spread * gradient[d] for d in range(3)]
    for batch in range(batches):
        fields[batch] = jnp.concatenate(
            [
                table[k][batch * halves + half : batch * halves + half + 1]
                for half in range(halves)
                for k in range(4)
            ],
            axis=0,
        )
    for owner in range(grid_size):
        staged[owner] = fields[asked[owner]]
    copies = []
    for step in range(1, grid_size):
        other = lax.rem(me + step, grid_size)
        copy = pltpu.make_async_remote_copy(
            src_ref=staged.at[other],
            dst_ref=out_ref.at[me],
            send_sem=send_c.at[step],
            recv_sem=recv_c.at[step],
            device_id=(other, col),
            device_id_type=MESH,
        )
        copy.start()
        copies.append(copy)
    extra[0] = valence
    extra[1] = point_scale * energy
    kept = fetch([(staged.at[me], out_ref.at[me]), (extra, extra_ref)], own_sem)
    for copy in copies:
        copy.wait_recv()
    for copy in sent + copies:
        copy.wait_send()
    for copy in kept:
        copy.wait()


def list_tiles(sizes, blocks_ref, tile_slot, tile_row, tile_col, started):
    grid_size, col_size, batches, row_blocks, halves = sizes
    me, col = lax.axis_index("grid"), lax.axis_index("col")
    entry = lax.div(me, grid_size // col_size)

    def step(slot, tiles):
        found = batch_of(blocks_ref, slot, entry, me, batches, row_blocks)
        batch = jnp.maximum(found, 0)
        has = found >= 0
        tile_slot[tiles] = slot
        tile_row[tiles] = blocks_ref[entry, slot * batches + batch]
        tile_col[tiles] = blocks_ref[col, slot * batches + batch]
        if started is not None:

            @pl.when(has)
            def _():
                started(tiles)

        return tiles + jnp.where(has, 1, 0)

    return lax.fori_loop(0, grid_size, step, jnp.int32(0), unroll=True)


def list_items(sizes, tiles, points_ref, tile_slot, item_tile, item_half):
    grid_size, col_size, batches, row_blocks, halves = sizes

    def step(tile, items):
        count = points_ref[jnp.where(tile < tiles, tile_slot[tile], 0), 3, 0]
        for half in range(halves):
            item_tile[items] = tile
            item_half[items] = half
            items = items + jnp.where((tile < tiles) & (count > half * BLK), 1, 0)
        return items

    return lax.fori_loop(0, grid_size, step, jnp.int32(0), unroll=True)


def half_rows(value, half, halves):
    picked = value[0:4]
    for other in range(1, halves):
        picked = jnp.where(half == other, value[4 * other : 4 * other + 4], picked)
    return picked


def functions_of(centres_ref, exponents_ref, row, column):
    rate = jnp.concatenate(
        [exponents_ref[pl.ds(row, 1), :], exponents_ref[pl.ds(column, 1), :]], axis=1
    )
    centre = jnp.concatenate(
        [
            centres_ref[:, pl.ds(pl.multiple_of(row * BLK, BLK), BLK)],
            centres_ref[:, pl.ds(pl.multiple_of(column * BLK, BLK), BLK)],
        ],
        axis=1,
    )
    return rate, centre


def distance_factors(points, rate, centre):
    square = jnp.sum(points * points, axis=0, keepdims=True)
    right = jnp.concatenate(
        [square, points, jnp.ones((1, BLK), F32), jnp.zeros((3, BLK), F32)], axis=0
    )
    left = jnp.concatenate(
        [
            -rate,
            2.0 * rate * centre,
            -rate * jnp.sum(centre * centre, axis=0, keepdims=True),
            jnp.zeros((3, 2 * BLK), F32),
        ],
        axis=0,
    )
    return right, left


def coefficients(rate, centre):
    lanes = lax.broadcasted_iota(jnp.int32, (1, 2 * BLK), 1)
    return jnp.concatenate(
        [
            rate,
            rate * centre,
            jnp.where(lanes >= BLK, 1.0, 0.0),
            jnp.zeros((3, 2 * BLK), F32),
        ],
        axis=0,
    )


def density_tiles(
    sizes,
    fills,
    blocks_hbm,
    density_ref,
    centres_hbm,
    exponents_hbm,
    points_hbm,
    sums_hbm,
    matrix_ref,
    sums_ref,
    out_sem,
    points_ref,
    blocks_ref,
    centres_ref,
    exponents_ref,
    fetch_sem,
    held,
    zeros,
    tile_slot,
    tile_row,
    tile_col,
    item_tile,
    item_half,
    tile_sem,
    fill_sem,
):
    grid_size, col_size, batches, row_blocks, halves = sizes
    col_blocks = density_ref.shape[1] // BLK
    first_row = lax.axis_index("grid") * row_blocks
    first_col = lax.axis_index("col") * col_blocks

    def tile_copy(tile):
        row = pl.multiple_of((tile_row[tile] - first_row) * BLK, BLK)
        column = pl.multiple_of((tile_col[tile] - first_col) * BLK, BLK)
        return pltpu.make_async_copy(
            density_ref.at[pl.ds(row, BLK), pl.ds(column, BLK)], held.at[tile], tile_sem.at[tile]
        )

    def fill_copy(index):
        return pltpu.make_async_copy(
            zeros, matrix_ref.at[pl.ds(index * FILL_ROWS, FILL_ROWS), :], fill_sem.at[index]
        )

    fetched = fetch(
        [
            (blocks_hbm, blocks_ref),
            (points_hbm, points_ref),
            (centres_hbm, centres_ref),
            (exponents_hbm, exponents_ref),
        ],
        fetch_sem,
    )
    zeros[...] = jnp.zeros_like(zeros)
    for index in range(fills):
        fill_copy(index).start()
    sums_ref[...] = jnp.zeros_like(sums_ref)
    fetched[0].wait()
    tiles = list_tiles(
        sizes, blocks_ref, tile_slot, tile_row, tile_col, lambda tile: tile_copy(tile).start()
    )
    fetched[1].wait()
    items = list_items(sizes, tiles, points_ref, tile_slot, item_tile, item_half)
    fetched[2].wait()
    fetched[3].wait()

    @pl.loop(0, tiles)
    def _(tile):
        tile_copy(tile).wait()

    def one(item):
        tile, half = item_tile[item], item_half[item]
        slot = tile_slot[tile]
        points = half_rows(points_ref[slot], half, halves)[0:3]
        rate, centre = functions_of(centres_ref, exponents_ref, tile_row[tile], tile_col[tile])
        right, left = distance_factors(points, rate, centre)
        value = jnp.exp(outer_sum(right, left))
        low = value.astype(BF16)
        panel = held[tile]
        left_sum = lax.dot_general(
            low[:, BLK:], panel, (((1,), (1,)), ((), ())), preferred_element_type=F32
        )
        right_sum = jnp.dot(low[:, :BLK], panel, preferred_element_type=F32)
        product = value * jnp.concatenate([left_sum, right_sum], axis=1)
        upper = product.astype(BF16)
        lower = (product - upper.astype(F32)).astype(BF16)
        c1, c2, c3 = parts_of(coefficients(rate, centre))
        rest = jnp.zeros((BLK - 24, 2 * BLK), F32)
        for_upper = jnp.concatenate([c1, c2, c3, rest], axis=0).astype(BF16)
        for_lower = jnp.concatenate([jnp.zeros_like(c1), c1, c2, rest], axis=0).astype(BF16)
        contract = (((1,), (1,)), ((), ()))
        terms = lax.dot_general(upper, for_upper, contract, preferred_element_type=F32)
        terms += lax.dot_general(lower, for_lower, contract, preferred_element_type=F32)
        terms = terms.T
        summed = terms[0:8] + terms[8:16] + terms[16:24]
        gradient = 2.0 * (summed[1:4] - points * summed[0:1])
        piece = jnp.concatenate([summed[4:5], gradient], axis=0)
        rows = lax.broadcasted_iota(jnp.int32, (4 * halves, BLK), 0)
        return slot, (rows >= 4 * half) & (rows < 4 * half + 4), jnp.concatenate([piece] * halves, 0)

    @pl.loop(0, lax.div(items + GROUP - 1, GROUP))
    def _(group):
        results = [one(jnp.minimum(GROUP * group + k, items - 1)) for k in range(GROUP)]
        for slot, chosen, piece in results:
            sums_ref[slot] = jnp.where(chosen, piece, sums_ref[slot])

    out = pltpu.make_async_copy(sums_ref, sums_hbm, out_sem)
    out.start()
    for index in range(fills):
        fill_copy(index).wait()
    out.wait()


def potential_tiles(
    sizes,
    fills,
    blocks_hbm,
    centres_hbm,
    exponents_hbm,
    points_hbm,
    fields_hbm,
    extra_hbm,
    given_ref,
    matrix_ref,
    samples_hbm,
    amounts_hbm,
    samples_ref,
    amounts_ref,
    out_sem,
    fields_ref,
    extra_ref,
    points_ref,
    blocks_ref,
    centres_ref,
    exponents_ref,
    fetch_sem,
    total,
    zeros,
    tile_slot,
    tile_row,
    tile_col,
    item_tile,
    item_half,
    tile_goal,
    first_at,
    tile_sem,
    fill_sem,
):
    grid_size, col_size, batches, row_blocks, halves = sizes
    row_count, col_count = matrix_ref.shape
    first_row = lax.axis_index("grid") * row_blocks
    first_col = lax.axis_index("col") * (col_count // BLK)

    def fill_copy(index):
        return pltpu.make_async_copy(
            zeros, matrix_ref.at[pl.ds(index * FILL_ROWS, FILL_ROWS), :], fill_sem.at[index]
        )

    fetched = fetch(
        [
            (blocks_hbm, blocks_ref),
            (points_hbm, points_ref),
            (centres_hbm, centres_ref),
            (exponents_hbm, exponents_ref),
            (fields_hbm, fields_ref),
            (extra_hbm, extra_ref),
        ],
        fetch_sem,
    )
    zeros[...] = jnp.zeros_like(zeros)
    every_fill = range(fills, row_count // FILL_ROWS)
    for index in every_fill:
        fill_copy(index).start()
    fetched[0].wait()
    tiles = list_tiles(sizes, blocks_ref, tile_slot, tile_row, tile_col, None)
    fetched[1].wait()
    items = list_items(sizes, tiles, points_ref, tile_slot, item_tile, item_half)
    total[...] = jnp.zeros_like(total)
    for copy in fetched[2:]:
        copy.wait()

    def place_of(tile):
        return (tile_row[tile] - first_row) * (col_count // BLK) + tile_col[tile] - first_col

    @pl.loop(0, tiles)
    def _(k):
        first_at[place_of(tiles - 1 - k)] = tiles - 1 - k

    @pl.loop(0, tiles)
    def _(tile):
        tile_goal[tile] = first_at[place_of(tile)]

    for batch in range(batches):
        for half in range(halves):
            place = batch * halves + half
            samples_ref[batch : batch + 1, half * BLK : (half + 1) * BLK] = extra_ref[
                0, place : place + 1, :
            ]
        amounts_ref[batch] = jnp.sum(extra_ref[1, batch * halves : (batch + 1) * halves, :])
    outs = fetch([(samples_ref, samples_hbm), (amounts_ref, amounts_hbm)], out_sem)

    def one(item):
        tile, half = item_tile[item], item_half[item]
        slot = tile_slot[tile]
        points = half_rows(points_ref[slot], half, halves)[0:3]
        field = half_rows(fields_ref[slot], half, halves)
        rate, centre = functions_of(centres_ref, exponents_ref, tile_row[tile], tile_col[tile])
        distance_right, distance_left = distance_factors(points, rate, centre)
        value = jnp.exp(outer_sum(distance_left, distance_right))
        slant = -2.0 * jnp.sum(field[1:4] * points, axis=0, keepdims=True)
        right = jnp.concatenate(
            [slant, 2.0 * field[1:4], field[0:1], jnp.zeros((3, BLK), F32)], axis=0
        )
        weighted = (value * outer_sum(coefficients(rate, centre), right)).astype(BF16)
        low = value.astype(BF16)
        left_side = jnp.concatenate([low[:BLK], weighted[:BLK]], axis=1)
        right_side = jnp.concatenate([weighted[BLK:], low[BLK:]], axis=1)
        return tile, lax.dot_general(
            left_side, right_side, (((1,), (1,)), ((), ())), preferred_element_type=F32
        )

    @pl.loop(0, lax.div(items + GROUP - 1, GROUP))
    def _(group):
        results = [one(jnp.minimum(GROUP * group + k, items - 1)) for k in range(GROUP)]
        for k, (tile, result) in enumerate(results):
            goal = jnp.where(GROUP * group + k < items, tile_goal[tile], grid_size)
            total[goal] += result


    def tile_copy(tile):
        row = pl.multiple_of((tile_row[tile] - first_row) * BLK, BLK)
        column = pl.multiple_of((tile_col[tile] - first_col) * BLK, BLK)
        return pltpu.make_async_copy(
            total.at[tile], matrix_ref.at[pl.ds(row, BLK), pl.ds(column, BLK)], tile_sem.at[tile]
        )

    def write_rows(first, last):
        @pl.loop(0, tiles)
        def _(tile):
            row = tile_row[tile] - first_row

            @pl.when((tile_goal[tile] == tile) & (row >= first) & (row < last))
            def _():
                tile_copy(tile).start()

    per_block = BLK // FILL_ROWS
    ready = fills // per_block
    write_rows(0, ready)
    for block in range(ready, row_blocks):
        for index in range(max(block * per_block, fills), (block + 1) * per_block):
            fill_copy(index).wait()
        if block % 2 == 1 or block == row_blocks - 1:
            write_rows(max(ready, block - block % 2), block + 1)

    @pl.loop(0, tiles)
    def _(tile):
        @pl.when(tile_goal[tile] == tile)
        def _():
            tile_copy(tile).wait()

    for copy in outs:
        copy.wait()


def local(density, centres, exponents, coords, weights, core_density, counts, blocks):
    grid_size = lax.axis_size("grid")
    col_size = lax.axis_size("col")
    row_count, col_count = density.shape
    batches, _, points_len = coords.shape
    row_blocks = row_count // BLK
    halves = points_len // BLK
    sizes = (grid_size, col_size, batches, row_blocks, halves)
    rates = exponents.reshape(exponents.shape[0] // BLK, BLK)
    table = blocks.T
    parts_first = coords.transpose(1, 0, 2)
    vmem = pl.BlockSpec(memory_space=pltpu.VMEM)
    smem = pl.BlockSpec(memory_space=pltpu.SMEM)
    anywhere = pl.BlockSpec(memory_space=pl.ANY)
    slot_shape = (grid_size, 4 * halves, BLK)
    hbm = pl.BlockSpec(memory_space=pltpu.HBM)
    table_memory = pltpu.SMEM(table.shape, jnp.int32)
    count_memory = pltpu.SMEM((batches,), jnp.int32)
    function_memory = [
        pltpu.VMEM(slot_shape, F32),
        table_memory,
        pltpu.VMEM(centres.shape, F32),
        pltpu.VMEM(rates.shape, F32),
        pltpu.SemaphoreType.DMA((6,)),
    ]
    slots = jax.ShapeDtypeStruct(slot_shape, F32)
    matrix = jax.ShapeDtypeStruct((row_count, col_count), F32)
    all_fills = row_count // FILL_ROWS
    fills = int(all_fills * FIRST_FILL)

    points = pl.pallas_call(
        lambda *refs: exchange_points(sizes, *refs),
        out_shape=slots,
        in_specs=[hbm, hbm, hbm],
        out_specs=anywhere,
        scratch_shapes=[
            table_memory,
            count_memory,
            pltpu.VMEM(parts_first.shape, F32),
            pltpu.VMEM((batches, 4 * halves, BLK), F32),
            pltpu.VMEM(slot_shape, F32),
            pltpu.SemaphoreType.DMA((3,)),
            pltpu.SemaphoreType.DMA,
            pltpu.SemaphoreType.DMA((grid_size,)),
            pltpu.SemaphoreType.DMA((grid_size,)),
        ],
        compiler_params=pltpu.CompilerParams(
            collective_id=0, has_side_effects=True, vmem_limit_bytes=VMEM_LIMIT
        ),
        name="exchange_points",
    )(table, counts, parts_first)

    lists = [pltpu.SMEM((grid_size + 1,), jnp.int32)] * 3 + [
        pltpu.SMEM((halves * grid_size + 1,), jnp.int32)
    ] * 2
    sums, started = pl.pallas_call(
        lambda *refs: density_tiles(sizes, fills, *refs),
        out_shape=(slots, matrix),
        in_specs=[hbm] * 5,
        out_specs=(anywhere, anywhere),
        scratch_shapes=[
            pltpu.VMEM(slot_shape, F32),
            pltpu.SemaphoreType.DMA,
            *function_memory,
            pltpu.VMEM((grid_size, BLK, BLK), BF16),
            pltpu.VMEM((FILL_ROWS, col_count), F32),
            *lists,
            pltpu.SemaphoreType.DMA((grid_size,)),
            pltpu.SemaphoreType.DMA((all_fills,)),
        ],
        compiler_params=pltpu.CompilerParams(vmem_limit_bytes=VMEM_LIMIT),
        name="density_tiles",
    )(table, density, centres, rates, points)

    fields, extra = pl.pallas_call(
        lambda *refs: exchange_sums(sizes, *refs),
        out_shape=(slots, jax.ShapeDtypeStruct((2, batches * halves, BLK), F32)),
        in_specs=[hbm, hbm, hbm, hbm, hbm],
        out_specs=(anywhere, anywhere),
        scratch_shapes=[
            pltpu.VMEM(slot_shape, F32),
            table_memory,
            count_memory,
            pltpu.VMEM(weights.shape, F32),
            pltpu.VMEM(core_density.shape, F32),
            pltpu.SemaphoreType.DMA((5,)),
            pltpu.VMEM(slot_shape, F32),
            pltpu.VMEM((col_size, batches, 4 * halves, BLK), F32),
            pltpu.VMEM((batches, 4 * halves, BLK), F32),
            pltpu.VMEM(slot_shape, F32),
            pltpu.VMEM((2, batches * halves, BLK), F32),
            pltpu.SemaphoreType.DMA((2,)),
            pltpu.SemaphoreType.DMA((grid_size,)),
            pltpu.SemaphoreType.DMA((grid_size,)),
            pltpu.SemaphoreType.DMA((col_size,)),
            pltpu.SemaphoreType.DMA((col_size,)),
            pltpu.SemaphoreType.DMA((grid_size,)),
            pltpu.SemaphoreType.DMA((grid_size,)),
        ],
        compiler_params=pltpu.CompilerParams(
            collective_id=1, has_side_effects=True, vmem_limit_bytes=VMEM_LIMIT
        ),
        name="exchange_sums",
    )(table, counts, weights, core_density, sums)

    return pl.pallas_call(
        lambda *refs: potential_tiles(sizes, fills, *refs),
        out_shape=(
            matrix,
            jax.ShapeDtypeStruct((batches, points_len), F32),
            jax.ShapeDtypeStruct((batches,), F32),
        ),
        in_specs=[hbm] * 6 + [anywhere],
        out_specs=(anywhere, anywhere, anywhere),
        scratch_shapes=[
            pltpu.VMEM((batches, points_len), F32),
            pltpu.SMEM((batches,), F32),
            pltpu.SemaphoreType.DMA((2,)),
            pltpu.VMEM(slot_shape, F32),
            pltpu.VMEM((2, batches * halves, BLK), F32),
            *function_memory,
            pltpu.VMEM((grid_size + 1, BLK, BLK), F32),
            pltpu.VMEM((FILL_ROWS, col_count), F32),
            *lists,
            pltpu.SMEM((grid_size + 1,), jnp.int32),
            pltpu.SMEM((row_blocks * (col_count // BLK),), jnp.int32),
            pltpu.SemaphoreType.DMA((grid_size,)),
            pltpu.SemaphoreType.DMA((all_fills,)),
        ],
        input_output_aliases={6: 0},
        compiler_params=pltpu.CompilerParams(vmem_limit_bytes=VMEM_LIMIT),
        name="potential_tiles",
    )(table, centres, rates, points, fields, extra, started)


def solution(mesh):
    return jax.shard_map(
        local,
        mesh=mesh,
        in_specs=(
            P("grid", "col"),
            P(),
            P(),
            P("grid", None, None),
            P("grid", None),
            P("grid", None),
            P("grid"),
            P(),
        ),
        out_specs=(P("grid", "col"), P("grid", None), P("grid")),
        check_vma=False,
    )
```

```python
import math

import jax
import jax.numpy as jnp
from jax import lax
from jax.experimental import pallas as pl
from jax.experimental.pallas import tpu as pltpu
from jax.sharding import PartitionSpec as P

BLK = 128
FILL_ROWS = 32
FIRST_FILL = 0.6
GROUP = 4
VMEM_LIMIT = 64 * 1024 * 1024
MESH = pl.DeviceIdType.MESH
F32 = jnp.float32
BF16 = jnp.bfloat16

kappa_pbe = 0.804
mu_coef = 0.2195
slater = -0.7385587663820224
grad_scale = 4.0 * (3.0 * math.pi**2) ** (2.0 / 3.0)
soft_square = 0.25


def xc_kernel(total, grad_square):
    root = jnp.sqrt(total * total + soft_square)
    regular = 0.5 * (total + root)
    log_regular = jnp.log(regular)
    third = jnp.exp(log_regular * (1.0 / 3.0))
    four_thirds = jnp.exp(log_regular * (4.0 / 3.0))
    scaled = grad_scale * four_thirds * four_thirds
    inverse = 1.0 / (kappa_pbe * scaled + mu_coef * grad_square)
    ratio = scaled * inverse
    enhance = 1.0 + kappa_pbe - kappa_pbe * kappa_pbe * ratio
    energy = slater * four_thirds * enhance
    inner = (4.0 / 3.0) * enhance - (8.0 / 3.0) * kappa_pbe * kappa_pbe * ratio * (
        mu_coef * grad_square * inverse
    )
    deriv_density = slater * third * inner * (0.5 * (1.0 + total / root))
    deriv_sigma = slater * four_thirds * (kappa_pbe * kappa_pbe * mu_coef) * ratio * inverse
    return energy, deriv_density, deriv_sigma


def parts_of(value):
    first = value.astype(BF16).astype(F32)
    rest = value - first
    second = rest.astype(BF16).astype(F32)
    return first, second, rest - second


def outer_sum(left, right):
    l1, l2, l3 = parts_of(left)
    r1, r2, r3 = parts_of(right)
    lefts = jnp.concatenate([l1, l1, l1, l2, l2, l3], axis=0).astype(BF16)
    rights = jnp.concatenate([r1, r2, r3, r1, r2, r1], axis=0).astype(BF16)
    return lax.dot_general(
        lefts, rights, (((0,), (0,)), ((), ())), preferred_element_type=F32
    )


def batch_of(blocks_ref, requester, entry, owner, batches, row_blocks):
    found = jnp.int32(-1)
    for batch in range(batches):
        offset = blocks_ref[entry, requester * batches + batch] - owner * row_blocks
        found = jnp.where((offset >= 0) & (offset < row_blocks), batch, found)
    return found


def owners_of(sizes, blocks_ref, requester):
    grid_size, col_size, batches, row_blocks, halves = sizes
    return [
        [lax.div(blocks_ref[entry, requester * batches + batch], row_blocks) for batch in range(batches)]
        for entry in range(col_size)
    ]


def asked_batch(sizes, owners, owner):
    grid_size, col_size, batches, row_blocks, halves = sizes
    found = jnp.int32(0)
    for batch in range(1, batches):
        found = jnp.where(owners[owner // (grid_size // col_size)][batch] == owner, batch, found)
    return found


def fetch(pairs, sems):
    copies = [
        pltpu.make_async_copy(source, target, sems.at[place])
        for place, (source, target) in enumerate(pairs)
    ]
    for copy in copies:
        copy.start()
    return copies


def exchange_points(
    sizes,
    blocks_hbm,
    counts_hbm,
    coords_hbm,
    out_ref,
    blocks_ref,
    counts_ref,
    coords_ref,
    packed,
    staged,
    fetch_sem,
    own_sem,
    send,
    recv,
):
    grid_size, col_size, batches, row_blocks, halves = sizes
    me, col = lax.axis_index("grid"), lax.axis_index("col")
    barrier = pltpu.get_barrier_semaphore()
    for step in range(1, grid_size):
        other = lax.rem(me + step, grid_size)
        pl.semaphore_signal(barrier, inc=1, device_id=(other, col), device_id_type=MESH)
    fetched = fetch(
        [(blocks_hbm, blocks_ref), (counts_hbm, counts_ref), (coords_hbm, coords_ref)], fetch_sem
    )
    for copy in fetched:
        copy.wait()
    points = coords_ref[...]
    for batch in range(batches):
        count = jnp.full((1, BLK), counts_ref[batch].astype(F32), F32)
        pieces = []
        for half in range(halves):
            lanes = slice(half * BLK, (half + 1) * BLK)
            pieces += [points[d, batch : batch + 1, lanes] for d in range(3)] + [count]
        packed[batch] = jnp.concatenate(pieces, axis=0)
    owners = owners_of(sizes, blocks_ref, me)
    for owner in range(grid_size):
        staged[owner] = packed[asked_batch(sizes, owners, owner)]
    pl.semaphore_wait(barrier, grid_size - 1)
    copies = []
    for step in range(1, grid_size):
        other = lax.rem(me + step, grid_size)
        copy = pltpu.make_async_remote_copy(
            src_ref=staged.at[other],
            dst_ref=out_ref.at[me],
            send_sem=send.at[step],
            recv_sem=recv.at[step],
            device_id=(other, col),
            device_id_type=MESH,
        )
        copy.start()
        copies.append(copy)
    own = pltpu.make_async_copy(staged.at[me], out_ref.at[me], own_sem)
    own.start()
    for copy in copies:
        copy.wait_recv()
    for copy in copies:
        copy.wait_send()
    own.wait()


def exchange_sums(
    sizes,
    blocks_hbm,
    counts_hbm,
    weights_hbm,
    core_hbm,
    sums_hbm,
    out_ref,
    extra_ref,
    sums_ref,
    blocks_ref,
    counts_ref,
    weights_ref,
    core_ref,
    fetch_sem,
    landed,
    col_sums,
    fields,
    staged,
    extra,
    own_sem,
    send_a,
    recv_a,
    send_b,
    recv_b,
    send_c,
    recv_c,
):
    grid_size, col_size, batches, row_blocks, halves = sizes
    me, col = lax.axis_index("grid"), lax.axis_index("col")
    barrier = pltpu.get_barrier_semaphore()
    for step in range(1, grid_size):
        other = lax.rem(me + step, grid_size)
        pl.semaphore_signal(barrier, inc=1, device_id=(other, col), device_id_type=MESH)
    for step in range(1, col_size):
        other = lax.rem(col + step, col_size)
        pl.semaphore_signal(barrier, inc=1, device_id=(me, other), device_id_type=MESH)
    fetched = fetch(
        [
            (blocks_hbm, blocks_ref),
            (counts_hbm, counts_ref),
            (weights_hbm, weights_ref),
            (core_hbm, core_ref),
            (sums_hbm, sums_ref),
        ],
        fetch_sem,
    )
    for copy in fetched:
        copy.wait()
    owners = owners_of(sizes, blocks_ref, me)
    asked = [asked_batch(sizes, owners, owner) for owner in range(grid_size)]
    pl.semaphore_wait(barrier, grid_size + col_size - 2)

    copies = []
    for step in range(1, grid_size):
        other = lax.rem(me + step, grid_size)
        copy = pltpu.make_async_remote_copy(
            src_ref=sums_ref.at[other],
            dst_ref=landed.at[me],
            send_sem=send_a.at[step],
            recv_sem=recv_a.at[step],
            device_id=(other, col),
            device_id_type=MESH,
        )
        copy.start()
        copies.append(copy)
    kept = fetch([(sums_ref.at[me], landed.at[me])], own_sem)
    for copy in copies:
        copy.wait_recv()
    kept[0].wait()
    sent = copies

    for batch in range(batches):
        total = None
        for entry in range(col_size):
            term = landed[owners[entry][batch]]
            total = term if total is None else total + term
        col_sums[col, batch] = total
    copies = []
    for step in range(1, col_size):
        other = lax.rem(col + step, col_size)
        copy = pltpu.make_async_remote_copy(
            src_ref=col_sums.at[col],
            dst_ref=col_sums.at[col],
            send_sem=send_b.at[step],
            recv_sem=recv_b.at[step],
            device_id=(me, other),
            device_id_type=MESH,
        )
        copy.start()
        copies.append(copy)
    for copy in copies:
        copy.wait_recv()
    sent += copies
    summed = col_sums[0]
    for entry in range(1, col_size):
        summed = summed + col_sums[entry]

    places = [(batch, half) for batch in range(batches) for half in range(halves)]

    def rows_of(field):
        return jnp.concatenate(
            [summed[batch, 4 * half + field : 4 * half + field + 1] for batch, half in places],
            axis=0,
        )

    def rows_in(ref):
        value = ref[...]
        return jnp.concatenate(
            [value[batch : batch + 1, half * BLK : (half + 1) * BLK] for batch, half in places],
            axis=0,
        )

    lanes = lax.broadcasted_iota(jnp.int32, (1, BLK), 1)
    live = jnp.concatenate(
        [jnp.where(lanes + half * BLK < counts_ref[batch], 1.0, 0.0) for batch, half in places],
        axis=0,
    )
    valence = jnp.where(live > 0.0, rows_of(0), 0.0)
    gradient = [jnp.where(live > 0.0, rows_of(1 + d), 0.0) for d in range(3)]
    grad_square = (
        gradient[0] * gradient[0] + gradient[1] * gradient[1] + gradient[2] * gradient[2]
    )
    energy, deriv_density, deriv_sigma = xc_kernel(valence + rows_in(core_ref), grad_square)
    point_scale = rows_in(weights_ref) * live
    spread = 2.0 * point_scale * deriv_sigma
    table = [point_scale * deriv_density] + [spread * gradient[d] for d in range(3)]
    for batch in range(batches):
        fields[batch] = jnp.concatenate(
            [
                table[k][batch * halves + half : batch * halves + half + 1]
                for half in range(halves)
                for k in range(4)
            ],
            axis=0,
        )
    for owner in range(grid_size):
        staged[owner] = fields[asked[owner]]
    copies = []
    for step in range(1, grid_size):
        other = lax.rem(me + step, grid_size)
        copy = pltpu.make_async_remote_copy(
            src_ref=staged.at[other],
            dst_ref=out_ref.at[me],
            send_sem=send_c.at[step],
            recv_sem=recv_c.at[step],
            device_id=(other, col),
            device_id_type=MESH,
        )
        copy.start()
        copies.append(copy)
    extra[0] = valence
    extra[1] = point_scale * energy
    kept = fetch([(staged.at[me], out_ref.at[me]), (extra, extra_ref)], own_sem)
    for copy in copies:
        copy.wait_recv()
    for copy in sent + copies:
        copy.wait_send()
    for copy in kept:
        copy.wait()


def list_tiles(sizes, blocks_ref, tile_slot, tile_row, tile_col, started):
    grid_size, col_size, batches, row_blocks, halves = sizes
    me, col = lax.axis_index("grid"), lax.axis_index("col")
    entry = lax.div(me, grid_size // col_size)

    def step(slot, tiles):
        found = batch_of(blocks_ref, slot, entry, me, batches, row_blocks)
        batch = jnp.maximum(found, 0)
        has = found >= 0
        tile_slot[tiles] = slot
        tile_row[tiles] = blocks_ref[entry, slot * batches + batch]
        tile_col[tiles] = blocks_ref[col, slot * batches + batch]
        if started is not None:

            @pl.when(has)
            def _():
                started(tiles)

        return tiles + jnp.where(has, 1, 0)

    return lax.fori_loop(0, grid_size, step, jnp.int32(0), unroll=True)


def list_items(sizes, tiles, points_ref, tile_slot, item_tile, item_half):
    grid_size, col_size, batches, row_blocks, halves = sizes

    def step(tile, items):
        count = points_ref[jnp.where(tile < tiles, tile_slot[tile], 0), 3, 0]
        for half in range(halves):
            item_tile[items] = tile
            item_half[items] = half
            items = items + jnp.where((tile < tiles) & (count > half * BLK), 1, 0)
        return items

    return lax.fori_loop(0, grid_size, step, jnp.int32(0), unroll=True)


def half_rows(value, half, halves):
    picked = value[0:4]
    for other in range(1, halves):
        picked = jnp.where(half == other, value[4 * other : 4 * other + 4], picked)
    return picked


def functions_of(centres_ref, exponents_ref, row, column):
    rate = jnp.concatenate(
        [exponents_ref[pl.ds(row, 1), :], exponents_ref[pl.ds(column, 1), :]], axis=1
    )
    centre = jnp.concatenate(
        [
            centres_ref[:, pl.ds(pl.multiple_of(row * BLK, BLK), BLK)],
            centres_ref[:, pl.ds(pl.multiple_of(column * BLK, BLK), BLK)],
        ],
        axis=1,
    )
    return rate, centre


def distance_factors(points, rate, centre):
    square = jnp.sum(points * points, axis=0, keepdims=True)
    right = jnp.concatenate(
        [square, points, jnp.ones((1, BLK), F32), jnp.zeros((3, BLK), F32)], axis=0
    )
    left = jnp.concatenate(
        [
            -rate,
            2.0 * rate * centre,
            -rate * jnp.sum(centre * centre, axis=0, keepdims=True),
            jnp.zeros((3, 2 * BLK), F32),
        ],
        axis=0,
    )
    return right, left


def coefficients(rate, centre):
    lanes = lax.broadcasted_iota(jnp.int32, (1, 2 * BLK), 1)
    return jnp.concatenate(
        [
            rate,
            rate * centre,
            jnp.where(lanes >= BLK, 1.0, 0.0),
            jnp.zeros((3, 2 * BLK), F32),
        ],
        axis=0,
    )


def density_tiles(
    sizes,
    fills,
    blocks_hbm,
    density_ref,
    centres_hbm,
    exponents_hbm,
    points_hbm,
    sums_hbm,
    matrix_ref,
    sums_ref,
    out_sem,
    points_ref,
    blocks_ref,
    centres_ref,
    exponents_ref,
    fetch_sem,
    held,
    zeros,
    tile_slot,
    tile_row,
    tile_col,
    item_tile,
    item_half,
    tile_sem,
    fill_sem,
):
    grid_size, col_size, batches, row_blocks, halves = sizes
    col_blocks = density_ref.shape[1] // BLK
    first_row = lax.axis_index("grid") * row_blocks
    first_col = lax.axis_index("col") * col_blocks

    def tile_copy(tile):
        row = pl.multiple_of((tile_row[tile] - first_row) * BLK, BLK)
        column = pl.multiple_of((tile_col[tile] - first_col) * BLK, BLK)
        return pltpu.make_async_copy(
            density_ref.at[pl.ds(row, BLK), pl.ds(column, BLK)], held.at[tile], tile_sem.at[tile]
        )

    def fill_copy(index):
        return pltpu.make_async_copy(
            zeros, matrix_ref.at[pl.ds(index * FILL_ROWS, FILL_ROWS), :], fill_sem.at[index]
        )

    fetched = fetch(
        [
            (blocks_hbm, blocks_ref),
            (points_hbm, points_ref),
            (centres_hbm, centres_ref),
            (exponents_hbm, exponents_ref),
        ],
        fetch_sem,
    )
    zeros[...] = jnp.zeros_like(zeros)
    for index in range(fills):
        fill_copy(index).start()
    sums_ref[...] = jnp.zeros_like(sums_ref)
    fetched[0].wait()
    tiles = list_tiles(
        sizes, blocks_ref, tile_slot, tile_row, tile_col, lambda tile: tile_copy(tile).start()
    )
    fetched[1].wait()
    items = list_items(sizes, tiles, points_ref, tile_slot, item_tile, item_half)
    fetched[2].wait()
    fetched[3].wait()

    @pl.loop(0, tiles)
    def _(tile):
        tile_copy(tile).wait()

    def one(item):
        tile, half = item_tile[item], item_half[item]
        slot = tile_slot[tile]
        points = half_rows(points_ref[slot], half, halves)[0:3]
        rate, centre = functions_of(centres_ref, exponents_ref, tile_row[tile], tile_col[tile])
        right, left = distance_factors(points, rate, centre)
        value = jnp.exp(outer_sum(right, left))
        low = value.astype(BF16)
        panel = held[tile]
        left_sum = lax.dot_general(
            low[:, BLK:], panel, (((1,), (1,)), ((), ())), preferred_element_type=F32
        )
        right_sum = jnp.dot(low[:, :BLK], panel, preferred_element_type=F32)
        product = value * jnp.concatenate([left_sum, right_sum], axis=1)
        upper = product.astype(BF16)
        lower = (product - upper.astype(F32)).astype(BF16)
        c1, c2, c3 = parts_of(coefficients(rate, centre))
        rest = jnp.zeros((BLK - 24, 2 * BLK), F32)
        for_upper = jnp.concatenate([c1, c2, c3, rest], axis=0).astype(BF16)
        for_lower = jnp.concatenate([jnp.zeros_like(c1), c1, c2, rest], axis=0).astype(BF16)
        contract = (((1,), (1,)), ((), ()))
        terms = lax.dot_general(upper, for_upper, contract, preferred_element_type=F32)
        terms += lax.dot_general(lower, for_lower, contract, preferred_element_type=F32)
        terms = terms.T
        summed = terms[0:8] + terms[8:16] + terms[16:24]
        gradient = 2.0 * (summed[1:4] - points * summed[0:1])
        piece = jnp.concatenate([summed[4:5], gradient], axis=0)
        rows = lax.broadcasted_iota(jnp.int32, (4 * halves, BLK), 0)
        return slot, (rows >= 4 * half) & (rows < 4 * half + 4), jnp.concatenate([piece] * halves, 0)

    @pl.loop(0, lax.div(items + GROUP - 1, GROUP))
    def _(group):
        results = [one(jnp.minimum(GROUP * group + k, items - 1)) for k in range(GROUP)]
        for slot, chosen, piece in results:
            sums_ref[slot] = jnp.where(chosen, piece, sums_ref[slot])

    out = pltpu.make_async_copy(sums_ref, sums_hbm, out_sem)
    out.start()
    for index in range(fills):
        fill_copy(index).wait()
    out.wait()


def potential_tiles(
    sizes,
    fills,
    blocks_hbm,
    centres_hbm,
    exponents_hbm,
    points_hbm,
    fields_hbm,
    extra_hbm,
    given_ref,
    matrix_ref,
    samples_hbm,
    amounts_hbm,
    samples_ref,
    amounts_ref,
    out_sem,
    fields_ref,
    extra_ref,
    points_ref,
    blocks_ref,
    centres_ref,
    exponents_ref,
    fetch_sem,
    total,
    zeros,
    tile_slot,
    tile_row,
    tile_col,
    item_tile,
    item_half,
    tile_goal,
    first_at,
    tile_sem,
    fill_sem,
):
    grid_size, col_size, batches, row_blocks, halves = sizes
    row_count, col_count = matrix_ref.shape
    first_row = lax.axis_index("grid") * row_blocks
    first_col = lax.axis_index("col") * (col_count // BLK)

    def fill_copy(index):
        return pltpu.make_async_copy(
            zeros, matrix_ref.at[pl.ds(index * FILL_ROWS, FILL_ROWS), :], fill_sem.at[index]
        )

    fetched = fetch(
        [
            (blocks_hbm, blocks_ref),
            (points_hbm, points_ref),
            (centres_hbm, centres_ref),
            (exponents_hbm, exponents_ref),
            (fields_hbm, fields_ref),
            (extra_hbm, extra_ref),
        ],
        fetch_sem,
    )
    zeros[...] = jnp.zeros_like(zeros)
    every_fill = range(fills, row_count // FILL_ROWS)
    for index in every_fill:
        fill_copy(index).start()
    fetched[0].wait()
    tiles = list_tiles(sizes, blocks_ref, tile_slot, tile_row, tile_col, None)
    fetched[1].wait()
    items = list_items(sizes, tiles, points_ref, tile_slot, item_tile, item_half)
    total[...] = jnp.zeros_like(total)
    for copy in fetched[2:]:
        copy.wait()

    def place_of(tile):
        return (tile_row[tile] - first_row) * (col_count // BLK) + tile_col[tile] - first_col

    @pl.loop(0, tiles)
    def _(k):
        first_at[place_of(tiles - 1 - k)] = tiles - 1 - k

    @pl.loop(0, tiles)
    def _(tile):
        tile_goal[tile] = first_at[place_of(tile)]

    for batch in range(batches):
        for half in range(halves):
            place = batch * halves + half
            samples_ref[batch : batch + 1, half * BLK : (half + 1) * BLK] = extra_ref[
                0, place : place + 1, :
            ]
        amounts_ref[batch] = jnp.sum(extra_ref[1, batch * halves : (batch + 1) * halves, :])
    outs = fetch([(samples_ref, samples_hbm), (amounts_ref, amounts_hbm)], out_sem)

    def one(item):
        tile, half = item_tile[item], item_half[item]
        slot = tile_slot[tile]
        points = half_rows(points_ref[slot], half, halves)[0:3]
        field = half_rows(fields_ref[slot], half, halves)
        rate, centre = functions_of(centres_ref, exponents_ref, tile_row[tile], tile_col[tile])
        distance_right, distance_left = distance_factors(points, rate, centre)
        value = jnp.exp(outer_sum(distance_left, distance_right))
        slant = -2.0 * jnp.sum(field[1:4] * points, axis=0, keepdims=True)
        right = jnp.concatenate(
            [slant, 2.0 * field[1:4], field[0:1], jnp.zeros((3, BLK), F32)], axis=0
        )
        weighted = (value * outer_sum(coefficients(rate, centre), right)).astype(BF16)
        low = value.astype(BF16)
        left_side = jnp.concatenate([low[:BLK], weighted[:BLK]], axis=1)
        right_side = jnp.concatenate([weighted[BLK:], low[BLK:]], axis=1)
        return tile, lax.dot_general(
            left_side, right_side, (((1,), (1,)), ((), ())), preferred_element_type=F32
        )

    @pl.loop(0, lax.div(items + GROUP - 1, GROUP))
    def _(group):
        results = [one(jnp.minimum(GROUP * group + k, items - 1)) for k in range(GROUP)]
        for k, (tile, result) in enumerate(results):
            goal = jnp.where(GROUP * group + k < items, tile_goal[tile], grid_size)
            total[goal] += result


    def tile_copy(tile):
        row = pl.multiple_of((tile_row[tile] - first_row) * BLK, BLK)
        column = pl.multiple_of((tile_col[tile] - first_col) * BLK, BLK)
        return pltpu.make_async_copy(
            total.at[tile], matrix_ref.at[pl.ds(row, BLK), pl.ds(column, BLK)], tile_sem.at[tile]
        )

    def write_rows(first, last):
        @pl.loop(0, tiles)
        def _(tile):
            row = tile_row[tile] - first_row

            @pl.when((tile_goal[tile] == tile) & (row >= first) & (row < last))
            def _():
                tile_copy(tile).start()

    per_block = BLK // FILL_ROWS
    ready = fills // per_block
    write_rows(0, ready)
    for block in range(ready, row_blocks):
        for index in range(max(block * per_block, fills), (block + 1) * per_block):
            fill_copy(index).wait()
        if block % 2 == 1 or block == row_blocks - 1:
            write_rows(max(ready, block - block % 2), block + 1)

    @pl.loop(0, tiles)
    def _(tile):
        @pl.when(tile_goal[tile] == tile)
        def _():
            tile_copy(tile).wait()

    for copy in outs:
        copy.wait()


def local(density, centres, exponents, coords, weights, core_density, counts, blocks):
    grid_size = lax.axis_size("grid")
    col_size = lax.axis_size("col")
    row_count, col_count = density.shape
    batches, _, points_len = coords.shape
    row_blocks = row_count // BLK
    halves = points_len // BLK
    sizes = (grid_size, col_size, batches, row_blocks, halves)
    rates = exponents.reshape(exponents.shape[0] // BLK, BLK)
    table = blocks.T
    parts_first = coords.transpose(1, 0, 2)
    vmem = pl.BlockSpec(memory_space=pltpu.VMEM)
    smem = pl.BlockSpec(memory_space=pltpu.SMEM)
    anywhere = pl.BlockSpec(memory_space=pl.ANY)
    slot_shape = (grid_size, 4 * halves, BLK)
    hbm = pl.BlockSpec(memory_space=pltpu.HBM)
    table_memory = pltpu.SMEM(table.shape, jnp.int32)
    count_memory = pltpu.SMEM((batches,), jnp.int32)
    function_memory = [
        pltpu.VMEM(slot_shape, F32),
        table_memory,
        pltpu.VMEM(centres.shape, F32),
        pltpu.VMEM(rates.shape, F32),
        pltpu.SemaphoreType.DMA((6,)),
    ]
    slots = jax.ShapeDtypeStruct(slot_shape, F32)
    matrix = jax.ShapeDtypeStruct((row_count, col_count), F32)
    all_fills = row_count // FILL_ROWS
    fills = int(all_fills * FIRST_FILL)

    points = pl.pallas_call(
        lambda *refs: exchange_points(sizes, *refs),
        out_shape=slots,
        in_specs=[hbm, hbm, hbm],
        out_specs=anywhere,
        scratch_shapes=[
            table_memory,
            count_memory,
            pltpu.VMEM(parts_first.shape, F32),
            pltpu.VMEM((batches, 4 * halves, BLK), F32),
            pltpu.VMEM(slot_shape, F32),
            pltpu.SemaphoreType.DMA((3,)),
            pltpu.SemaphoreType.DMA,
            pltpu.SemaphoreType.DMA((grid_size,)),
            pltpu.SemaphoreType.DMA((grid_size,)),
        ],
        compiler_params=pltpu.CompilerParams(
            collective_id=0, has_side_effects=True, vmem_limit_bytes=VMEM_LIMIT
        ),
        name="exchange_points",
    )(table, counts, parts_first)

    lists = [pltpu.SMEM((grid_size + 1,), jnp.int32)] * 3 + [
        pltpu.SMEM((halves * grid_size + 1,), jnp.int32)
    ] * 2
    sums, started = pl.pallas_call(
        lambda *refs: density_tiles(sizes, fills, *refs),
        out_shape=(slots, matrix),
        in_specs=[hbm] * 5,
        out_specs=(anywhere, anywhere),
        scratch_shapes=[
            pltpu.VMEM(slot_shape, F32),
            pltpu.SemaphoreType.DMA,
            *function_memory,
            pltpu.VMEM((grid_size, BLK, BLK), BF16),
            pltpu.VMEM((FILL_ROWS, col_count), F32),
            *lists,
            pltpu.SemaphoreType.DMA((grid_size,)),
            pltpu.SemaphoreType.DMA((all_fills,)),
        ],
        compiler_params=pltpu.CompilerParams(vmem_limit_bytes=VMEM_LIMIT),
        name="density_tiles",
    )(table, density, centres, rates, points)

    fields, extra = pl.pallas_call(
        lambda *refs: exchange_sums(sizes, *refs),
        out_shape=(slots, jax.ShapeDtypeStruct((2, batches * halves, BLK), F32)),
        in_specs=[hbm, hbm, hbm, hbm, hbm],
        out_specs=(anywhere, anywhere),
        scratch_shapes=[
            pltpu.VMEM(slot_shape, F32),
            table_memory,
            count_memory,
            pltpu.VMEM(weights.shape, F32),
            pltpu.VMEM(core_density.shape, F32),
            pltpu.SemaphoreType.DMA((5,)),
            pltpu.VMEM(slot_shape, F32),
            pltpu.VMEM((col_size, batches, 4 * halves, BLK), F32),
            pltpu.VMEM((batches, 4 * halves, BLK), F32),
            pltpu.VMEM(slot_shape, F32),
            pltpu.VMEM((2, batches * halves, BLK), F32),
            pltpu.SemaphoreType.DMA((2,)),
            pltpu.SemaphoreType.DMA((grid_size,)),
            pltpu.SemaphoreType.DMA((grid_size,)),
            pltpu.SemaphoreType.DMA((col_size,)),
            pltpu.SemaphoreType.DMA((col_size,)),
            pltpu.SemaphoreType.DMA((grid_size,)),
            pltpu.SemaphoreType.DMA((grid_size,)),
        ],
        compiler_params=pltpu.CompilerParams(
            collective_id=1, has_side_effects=True, vmem_limit_bytes=VMEM_LIMIT
        ),
        name="exchange_sums",
    )(table, counts, weights, core_density, sums)

    return pl.pallas_call(
        lambda *refs: potential_tiles(sizes, fills, *refs),
        out_shape=(
            matrix,
            jax.ShapeDtypeStruct((batches, points_len), F32),
            jax.ShapeDtypeStruct((batches,), F32),
        ),
        in_specs=[hbm] * 6 + [anywhere],
        out_specs=(anywhere, anywhere, anywhere),
        scratch_shapes=[
            pltpu.VMEM((batches, points_len), F32),
            pltpu.SMEM((batches,), F32),
            pltpu.SemaphoreType.DMA((2,)),
            pltpu.VMEM(slot_shape, F32),
            pltpu.VMEM((2, batches * halves, BLK), F32),
            *function_memory,
            pltpu.VMEM((grid_size + 1, BLK, BLK), F32),
            pltpu.VMEM((FILL_ROWS, col_count), F32),
            *lists,
            pltpu.SMEM((grid_size + 1,), jnp.int32),
            pltpu.SMEM((row_blocks * (col_count // BLK),), jnp.int32),
            pltpu.SemaphoreType.DMA((grid_size,)),
            pltpu.SemaphoreType.DMA((all_fills,)),
        ],
        input_output_aliases={6: 0},
        compiler_params=pltpu.CompilerParams(vmem_limit_bytes=VMEM_LIMIT),
        name="potential_tiles",
    )(table, centres, rates, points, fields, extra, started)


def solution(mesh):
    return jax.shard_map(
        local,
        mesh=mesh,
        in_specs=(
            P("grid", "col"),
            P(),
            P(),
            P("grid", None, None),
            P("grid", None),
            P("grid", None),
            P("grid"),
            P(),
        ),
        out_specs=(P("grid", "col"), P("grid", None), P("grid")),
        check_vma=False,
    )
```
